32 devices in a mesh: row: 8 (over z, y), col: 4 (over x, core).
Axes of the slice: x: 2, y: 2, z: 4, core: 2. Of those that a mesh axis runs over, the one named last changes fastest.
Arguments:
- panels: bfloat16 [16, 32, 128, 128], P('row', 'col'), may hold values from -0.26367188 to 0.26367188
- obs_of: int32 [16, 32], replicated, may hold values from 0 to 63, as said below
- counts: int32 [16], replicated, may hold values from 16 to 32, as said below
- inv_var: float32 [64, 128], replicated, may hold values from 0.25 to 4
- pattern: int32 [16, 16], replicated, may hold values from 0 to 1, as said below
- prior: float32 [2048, 2048], P('row', 'col'), may hold values from -2 to 2
Outputs:
- information: float32 [2048, 2048], P('row', 'col')
The draws below stay inside these ranges and needn't reach their ends.
Inputs may be any that keep to these rules, and one draw needn't show every extreme that they name: The 32 entries of a row of obs_of are distinct. `counts`: some panel has all 32 slots live. pattern is 1 on the diagonal and 0 below it.
All inputs are finite; a program needn't handle non-finite values.
Results may differ from the reference program's by a relative error of at most 0.0011.
Values may be sent and summed in bfloat16 or wider, within the bound.
A program may use at most 64 MiB of HBM per device.

```python
import math
import jax
import jax.numpy as jnp
from jax import lax

BS = 128
P_SIZE = 32
NB = 16
NOBS = 64


def draw_obs_of(key, part):
    row_keys = jax.random.split(jax.random.fold_in(key, 11), NB)
    rows_drawn = jax.vmap(lambda row_key: jax.random.permutation(row_key, NOBS)[:P_SIZE])(row_keys)
    return rows_drawn.astype(jnp.int32)


def draw_counts(key, part):
    key_vals = jax.random.fold_in(key, 21)
    key_full = jax.random.fold_in(key, 22)
    values = jax.random.randint(key_vals, (NB,), P_SIZE // 2, P_SIZE + 1)
    full_block = jax.random.randint(key_full, (), 0, NB)
    values = jnp.where(jnp.arange(NB) == full_block, P_SIZE, values)
    return values.astype(jnp.int32)


def draw_pattern(key, part):
    coin_flip = jax.random.randint(jax.random.fold_in(key, 31), (NB, NB), 0, 2)
    block_ids = jnp.arange(NB)
    diag_mask = block_ids[:, None] == block_ids[None, :]
    above_mask = block_ids[:, None] < block_ids[None, :]
    return jnp.where(diag_mask, 1, jnp.where(above_mask, coin_flip, 0)).astype(jnp.int32)


def block_levels(stream_key, extent, cuts, least, top_value):
    loudness = 1.0
    for axis_at, shards_of in cuts:
        steps = jax.random.uniform(jax.random.fold_in(jax.random.fold_in(stream_key, 6), axis_at), (shards_of,), jnp.float32, least / len(cuts), top_value / len(cuts))
        loudness = loudness * jnp.repeat(jnp.exp(steps), extent[axis_at] // shards_of).reshape((-1,) + (1,) * (len(extent) - 1 - axis_at))
    return loudness


def scatter_about(rng, extent, width, most, cuts=(), kind=jnp.bfloat16):
    result = jax.random.normal(rng, extent, jnp.float32) * width
    if len(cuts) > 0:
        result = block_levels(rng, extent, cuts, -0.22, 0.18) * result
    return jnp.clip(result, min=-most, max=most).astype(kind)


def setup_inputs(seed: int = 0) -> dict:
    splits = jax.random.split(jax.random.key(seed), 7)
    return {
        "panels": scatter_about(splits[0], (NB, P_SIZE, BS, BS), (0.5 / BS ** 0.5), 0.26367188, ((0, 8), (1, 4))),
        "obs_of": draw_obs_of(jax.random.fold_in(splits[6], 71), 0),
        "counts": draw_counts(jax.random.fold_in(splits[6], 71), 0),
        "inv_var": jnp.clip(jnp.exp(jax.random.uniform(splits[3], (NOBS, BS), jnp.float32, math.log(0.25), math.log(4.0))), 0.25, 4.0),
        "pattern": draw_pattern(jax.random.fold_in(splits[6], 71), 0),
        "prior": scatter_about(splits[5], (NB * BS, NB * BS), 0.3, 2.0, ((0, 8), (1, 4)), jnp.float32),
    }


def reference(panels, obs_of, counts, inv_var, pattern, prior):
    slot_ids = jnp.arange(P_SIZE, dtype=jnp.int32)
    live_slot = (slot_ids[None, :] < counts[:, None]).astype(jnp.float32)
    root_weight = jnp.sqrt(jnp.take(inv_var, obs_of, axis=0)) * live_slot[:, :, None]
    scaled = (panels.astype(jnp.float32) * root_weight[:, :, :, None]).astype(jnp.bfloat16)

    def pair_block(row_block, col_block):
        same_obs = obs_of[row_block][:, None] == obs_of[col_block][None, :]
        has_match = jnp.any(same_obs, axis=1)
        partner = lax.optimization_barrier(jnp.sum(jnp.where(same_obs, slot_ids[None, :], 0), axis=1)).astype(jnp.int32)
        picked = jnp.take(scaled[col_block], partner, axis=0).astype(jnp.float32)
        aligned = jnp.where(has_match[:, None, None], picked, jnp.zeros((), jnp.float32))
        return jnp.einsum('pax,pay->xy', scaled[row_block].astype(jnp.float32), aligned)

    def pair_step(carry, pair_index):
        row_block = pair_index // NB
        col_block = pair_index % NB
        pair_value = lax.cond(pattern[row_block, col_block] == 1, lambda: pair_block(row_block, col_block), lambda: jnp.zeros((BS, BS), jnp.float32))
        return (carry, pair_value)
    unused, blocks = lax.scan(pair_step, jnp.int32(0), jnp.arange(NB * NB, dtype=jnp.int32))
    upper_part = blocks.reshape(NB, NB, BS, BS)
    mirror_part = jnp.transpose(upper_part, (1, 0, 3, 2))
    block_ids = jnp.arange(NB, dtype=jnp.int32)
    lower_mask = (block_ids[:, None] > block_ids[None, :])[:, :, None, None]
    update = jnp.where(lower_mask, mirror_part, upper_part)
    return prior + jnp.transpose(update, (0, 2, 1, 3)).reshape(NB * BS, NB * BS)
```

```python
import functools

import jax
import jax.numpy as jnp
from jax import lax
from jax.experimental import pallas as pl
from jax.experimental.pallas import tpu as pltpu
from jax.sharding import PartitionSpec as P

MESH = pl.DeviceIdType.MESH


def gather_kernel(planes, fold, obs_ref, counts_ref, var_ref, panels_ref, rows_ref, cols_ref,
                  held, turned, z_send, z_recv, x_send, x_recv, y_send, y_recv, r_send, r_recv, keep):
    row, col = lax.axis_index("row"), lax.axis_index("col")
    plane, part = row // fold, row % fold
    groups, share = panels_ref.shape[0], panels_ref.shape[1]

    def at(other_row, other_col):
        return {"row": other_row, "col": other_col}

    def other_plane(step):
        return lax.rem(plane + step, planes)

    def other_col(step):
        return lax.rem(col + step, planes)

    def other_part(step):
        return lax.rem(part + step, fold)

    partners = [at(other_plane(s) * fold + part, col) for s in range(1, planes)]
    partners += [at(row, other_col(s)) for s in range(1, planes)]
    partners += [at(plane * fold + other_part(s), col) for s in range(1, fold)]
    barrier = pltpu.get_barrier_semaphore()
    for partner in partners:
        pl.semaphore_signal(barrier, inc=1, device_id=partner, device_id_type=MESH)

    weights = []
    for g in range(groups):
        block = row * groups + g
        for p in range(share):
            slot = col * share + p
            live = jnp.where(slot < counts_ref[block], 1.0, 0.0)
            weights.append(jnp.sqrt(var_ref[pl.ds(obs_ref[block, slot], 1), :]) * live)
    weights = jnp.concatenate(weights, axis=0).T
    for g in range(groups):
        for p in range(share):
            j = g * share + p
            scaled = panels_ref[g, p].astype(jnp.float32) * weights[:, j:j + 1]
            held[plane, g, p] = scaled.astype(jnp.bfloat16)
            turned[g, p] = scaled.T.astype(jnp.bfloat16)

    pl.semaphore_wait(barrier, len(partners))

    def z_copy(step, g, landing):
        return pltpu.make_async_remote_copy(
            src_ref=held.at[landing, g], dst_ref=held.at[landing, g],
            send_sem=z_send.at[step - 1, g], recv_sem=z_recv.at[landing, g],
            device_id=at(other_plane(step) * fold + part, col), device_id_type=MESH)

    def r_copy(step, landing):
        return pltpu.make_async_remote_copy(
            src_ref=turned, dst_ref=rows_ref.at[landing],
            send_sem=r_send.at[step - 1], recv_sem=r_recv.at[landing],
            device_id=at(row, other_col(step)), device_id_type=MESH)

    def x_copy(from_plane, g, landing):
        return pltpu.make_async_remote_copy(
            src_ref=held.at[from_plane, g], dst_ref=cols_ref.at[part, landing, g],
            send_sem=x_send.at[from_plane, g], recv_sem=x_recv.at[landing, g],
            device_id=at(row, from_plane), device_id_type=MESH)

    def y_copy(step, slot, g, landing):
        return pltpu.make_async_remote_copy(
            src_ref=cols_ref.at[landing, slot, g], dst_ref=cols_ref.at[landing, slot, g],
            send_sem=y_send.at[step - 1, slot, g], recv_sem=y_recv.at[landing, slot, g],
            device_id=at(plane * fold + other_part(step), col), device_id_type=MESH)

    def keep_copy(g):
        return pltpu.make_async_copy(held.at[col, g], cols_ref.at[part, col, g], keep.at[g])

    order = sorted(range(1, planes), key=lambda s: -min(s, planes - s))
    order = list(range(1, planes))
    for step in order:
        for g in range(groups):
            z_copy(step, g, plane).start()
    own_row = pltpu.make_async_copy(turned, rows_ref.at[col], keep.at[groups])
    own_row.start()

    def spread(from_plane):
        for g in range(groups):
            @pl.when(from_plane != col)
            def _():
                x_copy(from_plane, g, col).start()

            @pl.when(from_plane == col)
            def _():
                keep_copy(g).start()

    def forward(from_plane):
        @pl.when(from_plane == col)
        def _():
            for g in range(groups):
                keep_copy(g).wait()
                for step in range(1, fold):
                    y_copy(step, col, g, part).start()
            for s in range(1, planes):
                for g in range(groups):
                    x_copy(col, g, other_col(s)).wait_recv()
                    for step in range(1, fold):
                        y_copy(step, other_col(s), g, part).start()

    spread(plane)
    for step in range(1, planes):
        r_copy(step, col).start()
    before = plane
    for step in order:
        here = other_plane(step)
        for g in range(groups):
            z_copy(step, g, here).wait_recv()
        spread(here)
        forward(before)
        before = here
    forward(before)

    for step in range(1, planes):
        r_copy(step, other_col(step)).wait_recv()
    for step in range(1, fold):
        for slot in range(planes):
            for g in range(groups):
                y_copy(step, slot, g, other_part(step)).wait_recv()
    own_row.wait()
    for step in range(1, planes):
        r_copy(step, col).wait_send()
        for g in range(groups):
            z_copy(step, g, plane).wait_send()
            x_copy(other_col(step), g, col).wait_send()
    for step in range(1, fold):
        for slot in range(planes):
            for g in range(groups):
                y_copy(step, slot, g, part).wait_send()


def product_kernel(fold, width, place_ref, pattern_ref, rows_ref, cols_ref, prior_ref, out_ref, total):
    row, col = lax.axis_index("row"), lax.axis_index("col")
    groups, share, size = rows_ref.shape[1], rows_ref.shape[2], rows_ref.shape[3]
    block_cols = groups * fold
    observations = place_ref.shape[1]
    total[...] = jnp.zeros_like(total)
    zero = jnp.zeros((size, size), jnp.bfloat16)

    def step(i, unused):
        left, right = [], []
        for k in range(width):
            obs = i * width + k
            tiles = []
            for g in range(groups):
                slot = place_ref[row * groups + g, obs]
                safe = jnp.maximum(slot, 0)
                tile = rows_ref[safe // share, g, safe % share]
                tiles.append(jnp.where(slot >= 0, tile, zero))
            left.append(jnp.concatenate(tiles, axis=0))
            tiles = []
            for j in range(block_cols):
                slot = place_ref[col * block_cols + j, obs]
                safe = jnp.maximum(slot, 0)
                tile = cols_ref[j // groups, safe // share, j % groups, safe % share]
                tiles.append(jnp.where(slot >= 0, tile, zero))
            right.append(jnp.concatenate(tiles, axis=1))
        total[...] += jnp.dot(jnp.concatenate(left, axis=1), jnp.concatenate(right, axis=0),
                              preferred_element_type=jnp.float32)
        return unused

    lax.fori_loop(0, observations // width, step, 0)
    for g in range(groups):
        for j in range(block_cols):
            a, b = row * groups + g, col * block_cols + j
            kept = pattern_ref[jnp.minimum(a, b), jnp.maximum(a, b)] == 1
            across, down = pl.ds(g * size, size), pl.ds(j * size, size)
            out_ref[across, down] = prior_ref[across, down] + jnp.where(
                kept, total[across, down], 0.0)


def on_device(panels, obs_of, counts, inv_var, pattern, prior):
    planes = lax.axis_size("col")
    fold = lax.axis_size("row") // planes
    groups, share, size, _ = panels.shape
    observations = inv_var.shape[0]
    slots = jnp.arange(obs_of.shape[1], dtype=jnp.int32)
    found = obs_of[:, None, :] == jnp.arange(observations, dtype=jnp.int32)[None, :, None]
    place = jnp.max(jnp.where(found, slots[None, None, :], -1), axis=2)
    smem = pl.BlockSpec(memory_space=pltpu.SMEM)
    vmem = pl.BlockSpec(memory_space=pltpu.VMEM)
    dma = pltpu.SemaphoreType.DMA
    rows, cols = pl.pallas_call(
        functools.partial(gather_kernel, planes, fold),
        out_shape=(jax.ShapeDtypeStruct((planes, groups, share, size, size), jnp.bfloat16),
                   jax.ShapeDtypeStruct((fold, planes, groups, share, size, size), jnp.bfloat16)),
        in_specs=[smem, smem, vmem, vmem],
        out_specs=(vmem, vmem),
        scratch_shapes=[
            pltpu.VMEM((planes, groups, share, size, size), jnp.bfloat16),
            pltpu.VMEM((groups, share, size, size), jnp.bfloat16),
            dma((planes - 1, groups)), dma((planes, groups)),
            dma((planes, groups)), dma((planes, groups)),
            dma((max(fold - 1, 1), planes, groups)), dma((fold, planes, groups)),
            dma((planes - 1,)), dma((planes,)),
            dma((groups + 1,)),
        ],
        compiler_params=pltpu.CompilerParams(
            collective_id=0, has_side_effects=True, vmem_limit_bytes=48 * 1024 * 1024),
    )(obs_of, counts, inv_var, panels)
    return pl.pallas_call(
        functools.partial(product_kernel, fold, 4),
        out_shape=jax.ShapeDtypeStruct(prior.shape, prior.dtype),
        in_specs=[smem, smem, vmem, vmem, vmem],
        out_specs=vmem,
        scratch_shapes=[pltpu.VMEM(prior.shape, jnp.float32)],
        compiler_params=pltpu.CompilerParams(vmem_limit_bytes=48 * 1024 * 1024),
    )(place, pattern, rows, cols, prior)


def solution(mesh):
    placed = (P("row", "col", None, None), P(), P(), P(), P(), P("row", "col"))
    return jax.shard_map(
        on_device, mesh=mesh, in_specs=placed, out_specs=P("row", "col"), check_vma=False
    )
```

```python
import functools

import jax
import jax.numpy as jnp
from jax import lax
from jax.experimental import pallas as pl
from jax.experimental.pallas import tpu as pltpu
from jax.sharding import PartitionSpec as P

MESH = pl.DeviceIdType.MESH


def kernel(planes, fold, obs_ref, counts_ref, place_ref, pattern_ref, var_ref, panels_ref, prior_ref, out_ref,
           weights, leaving, held, turned, rows, cols, total, inbox,
           y_send, y_recv, z_send, z_recv, x_send, x_recv, r_send, r_recv, n_send, n_recv,
           t_send, t_recv, keep):
    row, col = lax.axis_index("row"), lax.axis_index("col")
    plane, part = row // fold, row % fold
    groups, share, size = panels_ref.shape[0], panels_ref.shape[1], panels_ref.shape[2]
    depth = size // fold
    wide = share * depth
    near = col + 1 - 2 * lax.rem(col, 2)
    far_steps = range(2, planes, 2)

    def at(other_row, other_col):
        return {"row": other_row, "col": other_col}

    def other_plane(step):
        return lax.rem(plane + step, planes)

    def other_col(step):
        return lax.rem(col + step, planes)

    def other_part(step):
        return lax.rem(part + step, fold)

    partners = [at(other_plane(s) * fold + part, col) for s in (1, planes - 1)]
    partners += [at(row, other_col(s)) for s in range(1, planes)]
    partners += [at(plane * fold + other_part(s), col) for s in range(1, fold)]
    barrier = pltpu.get_barrier_semaphore()
    for partner in partners:
        pl.semaphore_signal(barrier, inc=1, device_id=partner, device_id_type=MESH)

    factors = []
    for g in range(groups):
        block = row * groups + g
        for p in range(share):
            slot = col * share + p
            live = jnp.where(slot < counts_ref[block], 1.0, 0.0)
            factors.append(jnp.sqrt(var_ref[pl.ds(obs_ref[block, slot], 1), :]) * live)
    weights[...] = jnp.concatenate(factors, axis=0).T

    def scaled(to_part, g, p):
        j = g * share + p
        lines = pl.ds(pl.multiple_of(to_part * depth, depth), depth)
        value = panels_ref[g, p, lines, :].astype(jnp.float32) * weights[lines, j:j + 1]
        return value.astype(jnp.bfloat16)

    def copy(src, dst, send, recv, device):
        return pltpu.make_async_remote_copy(
            src_ref=src, dst_ref=dst, send_sem=send, recv_sem=recv,
            device_id=device, device_id_type=MESH)

    def y_copy(step, landing):
        return copy(leaving.at[step - 1], held.at[plane, landing], y_send.at[step - 1],
                    y_recv.at[landing], at(plane * fold + other_part(step), col))

    def z_copy(way, from_plane, chunk):
        target = lax.rem(plane + (1 if way == 0 else planes - 1), planes)
        return copy(held.at[from_plane, chunk], held.at[from_plane, chunk], z_send.at[way, from_plane, chunk],
                    z_recv.at[from_plane, chunk], at(target * fold + part, col))

    def x_copy(to_col, chunk, landing):
        return copy(held.at[to_col, chunk], cols.at[landing, chunk], x_send.at[to_col, chunk],
                    x_recv.at[landing, chunk], at(row, to_col))

    def keep_copy(chunk):
        return pltpu.make_async_copy(held.at[col, chunk], cols.at[col, chunk], keep.at[chunk])

    def far_copy(step, landing):
        return copy(turned, rows.at[landing], r_send.at[step], r_recv.at[landing], at(row, other_col(step)))

    def near_copy(slot, index, landing):
        source = turned if index == 0 else rows.at[slot]
        return copy(source, rows.at[landing], n_send.at[index], n_recv.at[index], at(row, near))

    def t_copy(step, g):
        return copy(total.at[other_part(step), g], inbox.at[step - 1, g], t_send.at[step - 1, g],
                    t_recv.at[step - 1, g], at(plane * fold + other_part(step), col))

    def spread(from_plane, chunk):
        @pl.when(from_plane != col)
        def _():
            x_copy(from_plane, chunk, col).start()

        @pl.when(from_plane == col)
        def _():
            keep_copy(chunk).start()

    def begin(chunk):
        @pl.when(plane < planes - 1)
        def _():
            z_copy(0, plane, chunk).start()

        @pl.when(plane > 0)
        def _():
            z_copy(1, plane, chunk).start()

        spread(plane, chunk)

    def turn(chunk):
        for g in range(groups):
            turned[chunk, g] = held[plane, chunk, g].reshape(wide, size).T

    for step in range(1, fold):
        for g in range(groups):
            for p in range(share):
                leaving[step - 1, g, p] = scaled(other_part(step), g, p)
    pl.semaphore_wait(barrier, len(partners))
    for step in range(1, fold):
        y_copy(step, part).start()
    for g in range(groups):
        for p in range(share):
            held[plane, part, g, p] = scaled(part, g, p)
    begin(part)
    turn(part)
    for step in range(1, fold):
        y_copy(step, other_part(step)).wait_recv()
        begin(other_part(step))
        turn(other_part(step))
    own_row = pltpu.make_async_copy(turned, rows.at[col], keep.at[fold])
    own_row.start()
    near_copy(col, 0, col).start()
    for step in far_steps:
        far_copy(step, col).start()

    def pass_rows():
        for index, step in enumerate(far_steps):
            slot = other_col(step)
            far_copy(step, slot).wait_recv()
            near_copy(slot, index + 1, slot).start()

    for step in range(1, planes):
        for order in range(fold):
            chunk = other_part(order)
            below, above = plane - step, plane + step

            @pl.when(below >= 0)
            def _():
                z_copy(0, below, chunk).wait_recv()

                @pl.when(plane < planes - 1)
                def _():
                    z_copy(0, below, chunk).start()

                spread(below, chunk)

            @pl.when(above < planes)
            def _():
                z_copy(1, above, chunk).wait_recv()

                @pl.when(plane > 0)
                def _():
                    z_copy(1, above, chunk).start()

                spread(above, chunk)
        if step == min(2, planes - 1):
            pass_rows()

    own_row.wait()
    near_copy(near, 0, near).wait_recv()
    for index, step in enumerate(far_steps):
        slot = lax.rem(near + step, planes)
        near_copy(slot, index + 1, slot).wait_recv()
    for chunk in range(fold):
        keep_copy(chunk).wait()
        for step in range(1, planes):
            x_copy(col, chunk, other_col(step)).wait_recv()

    zero = jnp.zeros((depth, size), jnp.bfloat16)
    block_cols = groups * fold

    def partial_tile(row_part, g):
        a = (plane * fold + row_part) * groups + g

        def step(slot_col, unused):
            lines = []
            for p in range(share):
                obs = obs_ref[a, slot_col * share + p]
                tiles = []
                for j in range(block_cols):
                    slot = place_ref[col * block_cols + j, obs]
                    safe = jnp.maximum(slot, 0)
                    tile = cols[safe // share, j // groups, j % groups, safe % share]
                    tiles.append(jnp.where(slot >= 0, tile, zero))
                lines.append(jnp.concatenate(tiles, axis=1))
            total[row_part, g] += jnp.dot(rows[slot_col, row_part, g], jnp.concatenate(lines, axis=0),
                                          preferred_element_type=jnp.float32)
            return unused

        total[row_part, g] = jnp.zeros(total.shape[2:], jnp.float32)
        lax.fori_loop(0, planes, step, 0)

    for step in range(1, fold):
        for g in range(groups):
            partial_tile(other_part(step), g)
            t_copy(step, g).start()
    for g in range(groups):
        partial_tile(part, g)

    for g in range(groups):
        update = total[part, g]
        for step in range(1, fold):
            t_copy(step, g).wait_recv()
            update = update + inbox[step - 1, g]
        across = pl.ds(g * size, size)
        for j in range(block_cols):
            a, b = row * groups + g, col * block_cols + j
            kept = pattern_ref[jnp.minimum(a, b), jnp.maximum(a, b)] == 1
            down = slice(j * size, (j + 1) * size)
            out_ref[across, down] = prior_ref[across, down] + jnp.where(
                kept, update[:, down], jnp.zeros((size, size), jnp.float32))

    for step in range(1, fold):
        y_copy(step, part).wait_send()
        for g in range(groups):
            t_copy(step, g).wait_send()
    for index in range(planes // 2):
        near_copy(col, index, col).wait_send()
    for step in far_steps:
        far_copy(step, col).wait_send()
    for chunk in range(fold):
        for step in range(1, planes):
            x_copy(other_col(step), chunk, col).wait_send()
        for from_plane in range(planes):
            @pl.when((from_plane <= plane) & (plane < planes - 1))
            def _():
                z_copy(0, from_plane, chunk).wait_send()

            @pl.when((from_plane >= plane) & (plane > 0))
            def _():
                z_copy(1, from_plane, chunk).wait_send()


def on_device(panels, obs_of, counts, inv_var, pattern, prior):
    planes = lax.axis_size("col")
    fold = lax.axis_size("row") // planes
    groups, share, size, _ = panels.shape
    depth = size // fold
    slots = jnp.arange(obs_of.shape[1], dtype=jnp.int32)
    ids = jnp.arange(inv_var.shape[0], dtype=jnp.int32)
    found = obs_of[:, None, :] == ids[None, :, None]
    place = jnp.max(jnp.where(found, slots[None, None, :], -1), axis=2)
    smem = pl.BlockSpec(memory_space=pltpu.SMEM)
    vmem = pl.BlockSpec(memory_space=pltpu.VMEM)
    dma = pltpu.SemaphoreType.DMA
    others = max(fold - 1, 1)
    panel = (fold, groups, share, depth, size)
    turned = (fold, groups, size, share * depth)
    tile = (groups, size, prior.shape[1])
    return pl.pallas_call(
        functools.partial(kernel, planes, fold),
        out_shape=jax.ShapeDtypeStruct(prior.shape, prior.dtype),
        in_specs=[smem, smem, smem, smem, vmem, vmem, vmem],
        out_specs=vmem,
        scratch_shapes=[
            pltpu.VMEM((size, groups * share), jnp.float32),
            pltpu.VMEM((others,) + panel[1:], jnp.bfloat16),
            pltpu.VMEM((planes,) + panel, jnp.bfloat16),
            pltpu.VMEM(turned, jnp.bfloat16),
            pltpu.VMEM((planes,) + turned, jnp.bfloat16),
            pltpu.VMEM((planes,) + panel, jnp.bfloat16),
            pltpu.VMEM((fold,) + tile, jnp.float32),
            pltpu.VMEM((others,) + tile, jnp.float32),
            dma((others,)), dma((fold,)),
            dma((2, planes, fold)), dma((planes, fold)),
            dma((planes, fold)), dma((planes, fold)),
            dma((planes,)), dma((planes,)),
            dma((planes // 2,)), dma((planes // 2,)),
            dma((others, groups)), dma((others, groups)),
            dma((fold + 1,)),
        ],
        compiler_params=pltpu.CompilerParams(
            collective_id=0, has_side_effects=True, vmem_limit_bytes=48 * 1024 * 1024),
    )(obs_of, counts, place, pattern, inv_var, panels, prior)


def solution(mesh):
    placed = (P("row", "col", None, None), P(), P(), P(), P(), P("row", "col"))
    return jax.shard_map(
        on_device, mesh=mesh, in_specs=placed, out_specs=P("row", "col"), check_vma=False
    )
```

```python
import functools

import jax
import jax.numpy as jnp
from jax import lax
from jax.experimental import pallas as pl
from jax.experimental.pallas import tpu as pltpu
from jax.sharding import PartitionSpec as P

MESH = pl.DeviceIdType.MESH


def kernel(planes, fold, obs_ref, counts_ref, place_ref, pattern_ref, var_ref, source_ref, out_ref,
           panels_ref, weights, leaving, held, turned, rows, cols, total, inbox,
           y_send, y_recv, z_send, z_recv, x_send, x_recv, r_send, r_recv, n_send, n_recv,
           t_send, t_recv, keep, fetch):
    row, col = lax.axis_index("row"), lax.axis_index("col")
    plane, part = row // fold, row % fold
    groups, share, size = panels_ref.shape[0], panels_ref.shape[1], panels_ref.shape[2]
    depth = size // fold
    wide = share * depth
    near = col + 1 - 2 * lax.rem(col, 2)
    far_steps = range(2, planes, 2)

    def at(other_row, other_col):
        return {"row": other_row, "col": other_col}

    def other_plane(step):
        return lax.rem(plane + step, planes)

    def other_col(step):
        return lax.rem(col + step, planes)

    def other_part(step):
        return lax.rem(part + step, fold)

    fetched = pltpu.make_async_copy(source_ref, panels_ref, fetch)
    fetched.start()
    partners = [at(other_plane(s) * fold + part, col) for s in (1, planes - 1)]
    partners += [at(row, other_col(s)) for s in range(1, planes)]
    partners += [at(plane * fold + other_part(s), col) for s in range(1, fold)]
    barrier = pltpu.get_barrier_semaphore()
    for partner in partners:
        pl.semaphore_signal(barrier, inc=1, device_id=partner, device_id_type=MESH)

    factors = []
    for g in range(groups):
        block = row * groups + g
        for p in range(share):
            slot = col * share + p
            live = jnp.where(slot < counts_ref[block], 1.0, 0.0)
            factors.append(jnp.sqrt(var_ref[pl.ds(obs_ref[block, slot], 1), :]) * live)
    weights[...] = jnp.concatenate(factors, axis=0).T
    fetched.wait()

    def scaled(to_part, g, p):
        j = g * share + p
        lines = pl.ds(pl.multiple_of(to_part * depth, depth), depth)
        value = panels_ref[g, p, lines, :].astype(jnp.float32) * weights[lines, j:j + 1]
        return value.astype(jnp.bfloat16)

    def copy(src, dst, send, recv, device):
        return pltpu.make_async_remote_copy(
            src_ref=src, dst_ref=dst, send_sem=send, recv_sem=recv,
            device_id=device, device_id_type=MESH)

    def y_copy(step, g, landing):
        return copy(leaving.at[step - 1, g], held.at[plane, landing, g], y_send.at[step - 1, g],
                    y_recv.at[landing, g], at(plane * fold + other_part(step), col))

    def z_copy(way, from_plane, chunk, g):
        target = lax.rem(plane + (1 if way == 0 else planes - 1), planes)
        return copy(held.at[from_plane, chunk, g], held.at[from_plane, chunk, g],
                    z_send.at[way, from_plane, chunk, g], z_recv.at[from_plane, chunk, g],
                    at(target * fold + part, col))

    def x_copy(to_col, order, g, landing):
        return copy(held.at[to_col, other_part(order), g], cols[order].at[landing, g],
                    x_send.at[to_col, order, g], x_recv.at[landing, order, g], at(row, to_col))

    def keep_copy(order, g):
        return pltpu.make_async_copy(held.at[col, other_part(order), g], cols[order].at[col, g],
                                     keep.at[order, g])

    def far_copy(step, landing):
        return copy(turned, rows.at[landing], r_send.at[step], r_recv.at[landing], at(row, other_col(step)))

    def near_copy(slot, index, landing):
        source = turned if index == 0 else rows.at[slot]
        return copy(source, rows.at[landing], n_send.at[index], n_recv.at[index], at(row, near))

    def t_copy(step, chunk, g):
        return copy(total.at[other_part(step), chunk, g], inbox.at[step - 1, chunk, g],
                    t_send.at[step - 1, chunk, g], t_recv.at[step - 1, chunk, g],
                    at(plane * fold + other_part(step), col))

    def spread(from_plane, order, g):
        @pl.when(from_plane != col)
        def _():
            x_copy(from_plane, order, g, col).start()

        @pl.when(from_plane == col)
        def _():
            keep_copy(order, g).start()

    def begin(chunk, g):
        @pl.when(plane < planes - 1)
        def _():
            z_copy(0, plane, chunk, g).start()

        @pl.when(plane > 0)
        def _():
            z_copy(1, plane, chunk, g).start()

    def turn(chunk, g):
        turned[chunk, g] = held[plane, chunk, g].reshape(wide, size).T

    for step in range(1, fold):
        for g in range(groups):
            for p in range(share):
                leaving[step - 1, g, p] = scaled(other_part(step), g, p)
    pl.semaphore_wait(barrier, len(partners))
    for step in range(1, fold):
        for g in range(groups):
            y_copy(step, g, part).start()
    for g in range(groups):
        for p in range(share):
            held[plane, part, g, p] = scaled(part, g, p)
        begin(part, g)
    for g in range(groups):
        spread(plane, 0, g)
        turn(part, g)
    for step in range(1, fold):
        for g in range(groups):
            y_copy(step, g, other_part(step)).wait_recv()
            begin(other_part(step), g)
        for g in range(groups):
            spread(plane, step, g)
            turn(other_part(step), g)
    own_row = pltpu.make_async_copy(turned, rows.at[col], fetch)
    own_row.start()
    near_copy(col, 0, col).start()
    for step in far_steps:
        far_copy(step, col).start()

    def pass_rows():
        for index, step in enumerate(far_steps):
            slot = other_col(step)
            far_copy(step, slot).wait_recv()
            near_copy(slot, index + 1, slot).start()

    for step in range(1, planes):
        below, above = plane - step, plane + step
        for order in range(fold):
            chunk = other_part(order)
            for g in range(groups):
                @pl.when(below >= 0)
                def _():
                    z_copy(0, below, chunk, g).wait_recv()

                    @pl.when(plane < planes - 1)
                    def _():
                        z_copy(0, below, chunk, g).start()

                    spread(below, order, g)

                @pl.when(above < planes)
                def _():
                    z_copy(1, above, chunk, g).wait_recv()

                    @pl.when(plane > 0)
                    def _():
                        z_copy(1, above, chunk, g).start()

                    spread(above, order, g)
        if step == min(2, planes - 1):
            pass_rows()

    own_row.wait()
    near_copy(near, 0, near).wait_recv()
    for index, step in enumerate(far_steps):
        slot = lax.rem(near + step, planes)
        near_copy(slot, index + 1, slot).wait_recv()
    zero = jnp.zeros((depth, size), jnp.bfloat16)
    block_cols = groups * fold

    def partial_tiles(row_part, order):
        chunk = other_part(order)

        def step(slot_col, unused):
            for g in range(groups):
                a = (plane * fold + row_part) * groups + g
                lines = []
                for p in range(share):
                    obs = obs_ref[a, slot_col * share + p]
                    tiles = []
                    for h in range(groups):
                        slot = place_ref[col * block_cols + chunk * groups + h, obs]
                        safe = jnp.maximum(slot, 0)
                        tile = cols[order][safe // share, h, safe % share]
                        tiles.append(jnp.where(slot >= 0, tile, zero))
                    lines.append(jnp.concatenate(tiles, axis=1))
                total[row_part, chunk, g] += jnp.dot(
                    rows[slot_col, row_part, g], jnp.concatenate(lines, axis=0),
                    preferred_element_type=jnp.float32)
            return unused

        total[row_part, chunk] = jnp.zeros(total.shape[2:], jnp.float32)
        lax.fori_loop(0, planes, step, 0)

    for order in range(fold):
        chunk = other_part(order)
        for g in range(groups):
            keep_copy(order, g).wait()
            for step in range(1, planes):
                x_copy(col, order, g, other_col(step)).wait_recv()
        for step in range(1, fold):
            partial_tiles(other_part(step), order)
            for g in range(groups):
                t_copy(step, chunk, g).start()
        partial_tiles(part, order)

    for order in range(fold):
        chunk = other_part(order)
        for g in range(groups):
            update = total[part, chunk, g]
            for step in range(1, fold):
                t_copy(step, chunk, g).wait_recv()
                update = update + inbox[step - 1, chunk, g]
            for h in range(groups):
                a, b = row * groups + g, col * block_cols + chunk * groups + h
                kept = pattern_ref[jnp.minimum(a, b), jnp.maximum(a, b)] == 1
                down = pl.ds(pl.multiple_of((chunk * groups + h) * size, size), size)
                out_ref[g * size:(g + 1) * size, down] = jnp.where(
                    kept, update[:, h * size:(h + 1) * size], jnp.zeros((size, size), jnp.float32))

    for step in range(1, fold):
        for g in range(groups):
            y_copy(step, g, part).wait_send()
            for chunk in range(fold):
                t_copy(step, chunk, g).wait_send()
    for index in range(planes // 2):
        near_copy(col, index, col).wait_send()
    for step in far_steps:
        far_copy(step, col).wait_send()
    for chunk in range(fold):
        for g in range(groups):
            for step in range(1, planes):
                x_copy(other_col(step), chunk, g, col).wait_send()
            for from_plane in range(planes):
                @pl.when((from_plane <= plane) & (plane < planes - 1))
                def _():
                    z_copy(0, from_plane, chunk, g).wait_send()

                @pl.when((from_plane >= plane) & (plane > 0))
                def _():
                    z_copy(1, from_plane, chunk, g).wait_send()


def on_device(panels, obs_of, counts, inv_var, pattern, prior):
    planes = lax.axis_size("col")
    fold = lax.axis_size("row") // planes
    groups, share, size, _ = panels.shape
    depth = size // fold
    slots = jnp.arange(obs_of.shape[1], dtype=jnp.int32)
    ids = jnp.arange(inv_var.shape[0], dtype=jnp.int32)
    found = obs_of[:, None, :] == ids[None, :, None]
    place = jnp.max(jnp.where(found, slots[None, None, :], -1), axis=2)
    smem = pl.BlockSpec(memory_space=pltpu.SMEM)
    vmem = pl.BlockSpec(memory_space=pltpu.VMEM)
    dma = pltpu.SemaphoreType.DMA
    others = max(fold - 1, 1)
    panel = (fold, groups, share, depth, size)
    turned = (fold, groups, size, share * depth)
    tile = (fold, groups, size, groups * size)
    update = pl.pallas_call(
        functools.partial(kernel, planes, fold),
        out_shape=jax.ShapeDtypeStruct(prior.shape, prior.dtype),
        in_specs=[smem, smem, smem, smem, vmem, pl.BlockSpec(memory_space=pl.ANY)],
        out_specs=vmem,
        scratch_shapes=[
            pltpu.VMEM(panels.shape, jnp.bfloat16),
            pltpu.VMEM((size, groups * share), jnp.float32),
            pltpu.VMEM((others,) + panel[1:], jnp.bfloat16),
            pltpu.VMEM((planes,) + panel, jnp.bfloat16),
            pltpu.VMEM(turned, jnp.bfloat16),
            pltpu.VMEM((planes,) + turned, jnp.bfloat16),
            (pltpu.VMEM((planes,) + panel[1:], jnp.bfloat16),) * fold,
            pltpu.VMEM((fold,) + tile, jnp.float32),
            pltpu.VMEM((others,) + tile, jnp.float32),
            dma((others, groups)), dma((fold, groups)),
            dma((2, planes, fold, groups)), dma((planes, fold, groups)),
            dma((planes, fold, groups)), dma((planes, fold, groups)),
            dma((planes,)), dma((planes,)),
            dma((planes // 2,)), dma((planes // 2,)),
            dma((others, fold, groups)), dma((others, fold, groups)),
            dma((fold, groups)), dma,
        ],
        compiler_params=pltpu.CompilerParams(
            collective_id=0, has_side_effects=True, vmem_limit_bytes=60 * 1024 * 1024),
    )(obs_of, counts, place, pattern, inv_var, panels)
    return prior + update


def solution(mesh):
    placed = (P("row", "col", None, None), P(), P(), P(), P(), P("row", "col"))
    return jax.shard_map(
        on_device, mesh=mesh, in_specs=placed, out_specs=P("row", "col"), check_vma=False
    )
```

```python
import functools

import jax
import jax.numpy as jnp
from jax import lax
from jax.experimental import pallas as pl
from jax.experimental.pallas import tpu as pltpu
from jax.sharding import PartitionSpec as P

MESH = pl.DeviceIdType.MESH


def kernel(planes, fold, obs_ref, counts_ref, pattern_ref, ids_ref, var_ref, source_ref, prior_source, out_ref,
           panels_ref, prior_ref, table, place_ref, weights, leaving, held, turned, rows, cols, total, inbox,
           y_send, y_recv, z_send, z_recv, x_send, x_recv, r_send, r_recv, n_send, n_recv,
           t_send, t_recv, keep, fetch, prior_fetch, place_fetch):
    row, col = lax.axis_index("row"), lax.axis_index("col")
    plane, part = row // fold, row % fold
    groups, share, size = panels_ref.shape[0], panels_ref.shape[1], panels_ref.shape[2]
    depth = size // fold
    wide = share * depth
    near = col + 1 - 2 * lax.rem(col, 2)
    far_steps = range(2, planes, 2)

    def at(other_row, other_col):
        return {"row": other_row, "col": other_col}

    def other_plane(step):
        return lax.rem(plane + step, planes)

    def other_col(step):
        return lax.rem(col + step, planes)

    def other_part(step):
        return lax.rem(part + step, fold)

    fetched = pltpu.make_async_copy(source_ref, panels_ref, fetch)
    fetched.start()
    prior_fetched = pltpu.make_async_copy(prior_source, prior_ref, prior_fetch)
    prior_fetched.start()
    partners = [at(other_plane(s) * fold + part, col) for s in (1, planes - 1)]
    partners += [at(row, other_col(s)) for s in range(1, planes)]
    partners += [at(plane * fold + other_part(s), col) for s in range(1, fold)]
    barrier = pltpu.get_barrier_semaphore()
    for partner in partners:
        pl.semaphore_signal(barrier, inc=1, device_id=partner, device_id_type=MESH)

    factors = []
    for g in range(groups):
        block = row * groups + g
        for p in range(share):
            slot = col * share + p
            live = jnp.where(slot < counts_ref[block], 1.0, 0.0)
            factors.append(jnp.sqrt(var_ref[pl.ds(obs_ref[block, slot], 1), :]) * live)
    weights[...] = jnp.concatenate(factors, axis=0).T
    fetched.wait()

    def scaled(to_part, g, p):
        j = g * share + p
        lines = pl.ds(pl.multiple_of(to_part * depth, depth), depth)
        value = panels_ref[g, p, lines, :].astype(jnp.float32) * weights[lines, j:j + 1]
        return value.astype(jnp.bfloat16)

    def copy(src, dst, send, recv, device):
        return pltpu.make_async_remote_copy(
            src_ref=src, dst_ref=dst, send_sem=send, recv_sem=recv,
            device_id=device, device_id_type=MESH)

    def y_copy(step, g, landing):
        return copy(leaving.at[step - 1, g], held.at[plane, landing, g], y_send.at[step - 1, g],
                    y_recv.at[landing, g], at(plane * fold + other_part(step), col))

    def z_copy(way, from_plane, chunk, g):
        target = lax.rem(plane + (1 if way == 0 else planes - 1), planes)
        return copy(held.at[from_plane, chunk, g], held.at[from_plane, chunk, g],
                    z_send.at[way, from_plane, chunk, g], z_recv.at[from_plane, chunk, g],
                    at(target * fold + part, col))

    def x_copy(to_col, order, g, landing):
        return copy(held.at[to_col, other_part(order), g], cols[order].at[landing, g],
                    x_send.at[to_col, order, g], x_recv.at[landing, order, g], at(row, to_col))

    def keep_copy(order, g):
        return pltpu.make_async_copy(held.at[col, other_part(order), g], cols[order].at[col, g],
                                     keep.at[order, g])

    def far_copy(step, landing):
        return copy(turned, rows.at[landing], r_send.at[step], r_recv.at[landing], at(row, other_col(step)))

    def near_copy(slot, index, landing):
        source = turned if index == 0 else rows.at[slot]
        return copy(source, rows.at[landing], n_send.at[index], n_recv.at[index], at(row, near))

    def t_copy(step, chunk, g):
        return copy(total.at[other_part(step), chunk, g], inbox.at[step - 1, chunk, g],
                    t_send.at[step - 1, chunk, g], t_recv.at[step - 1, chunk, g],
                    at(plane * fold + other_part(step), col))

    def spread(from_plane, order, g):
        @pl.when(from_plane != col)
        def _():
            x_copy(from_plane, order, g, col).start()

        @pl.when(from_plane == col)
        def _():
            keep_copy(order, g).start()

    def begin(chunk, g):
        @pl.when(plane < planes - 1)
        def _():
            z_copy(0, plane, chunk, g).start()

        @pl.when(plane > 0)
        def _():
            z_copy(1, plane, chunk, g).start()

    def turn(chunk, g):
        turned[chunk, g] = held[plane, chunk, g].reshape(wide, size).T

    for step in range(1, fold):
        for g in range(groups):
            for p in range(share):
                leaving[step - 1, g, p] = scaled(other_part(step), g, p)
    pl.semaphore_wait(barrier, len(partners))
    for step in range(1, fold):
        for g in range(groups):
            y_copy(step, g, part).start()
    for g in range(groups):
        for p in range(share):
            held[plane, part, g, p] = scaled(part, g, p)
        begin(part, g)
    for g in range(groups):
        spread(plane, 0, g)
        turn(part, g)
    for step in range(1, fold):
        for g in range(groups):
            y_copy(step, g, other_part(step)).wait_recv()
            begin(other_part(step), g)
        for g in range(groups):
            spread(plane, step, g)
            turn(other_part(step), g)
    ids = lax.broadcasted_iota(jnp.int32, table.shape, 1)
    found = jnp.full(table.shape, -1, jnp.int32)
    for p in range(ids_ref.shape[1]):
        found = jnp.where(ids_ref[:, p:p + 1] == ids, p, found)
    table[...] = found
    placed = pltpu.make_async_copy(table, place_ref, place_fetch)
    placed.start()
    own_row = pltpu.make_async_copy(turned, rows.at[col], fetch)
    own_row.start()
    near_copy(col, 0, col).start()
    for step in far_steps:
        far_copy(step, col).start()

    def pass_rows():
        for index, step in enumerate(far_steps):
            slot = other_col(step)
            far_copy(step, slot).wait_recv()
            near_copy(slot, index + 1, slot).start()

    zero = jnp.zeros((depth, size), jnp.bfloat16)
    block_cols = groups * fold

    def partial_tiles(step_part, order):
        row_part, chunk = other_part(step_part), other_part(order)

        def step(slot_col, unused):
            for g in range(groups):
                a = (plane * fold + row_part) * groups + g
                lines = []
                for p in range(share):
                    obs = obs_ref[a, slot_col * share + p]
                    tiles = []
                    for h in range(groups):
                        slot = place_ref[col * block_cols + chunk * groups + h, obs]
                        safe = jnp.maximum(slot, 0)
                        tile = cols[order][safe // share, h, safe % share]
                        tiles.append(jnp.where(slot >= 0, tile, zero))
                    lines.append(jnp.concatenate(tiles, axis=1))
                total[row_part, chunk, g] += jnp.dot(
                    rows[slot_col, row_part, g], jnp.concatenate(lines, axis=0),
                    preferred_element_type=jnp.float32)
            return unused

        total[row_part, chunk] = jnp.zeros(total.shape[2:], jnp.float32)
        lax.fori_loop(0, planes, step, 0)
        if step_part > 0:
            for g in range(groups):
                t_copy(step_part, chunk, g).start()

    def await_rows():
        placed.wait()
        own_row.wait()
        near_copy(near, 0, near).wait_recv()
        for index, step in enumerate(far_steps):
            slot = lax.rem(near + step, planes)
            near_copy(slot, index + 1, slot).wait_recv()

    def await_columns(order):
        for g in range(groups):
            keep_copy(order, g).wait()
            for step in range(1, planes):
                x_copy(col, order, g, other_col(step)).wait_recv()

    distance = jnp.maximum(plane - col, col - plane)
    units = [(step, order) for step in range(1, fold) for order in range(fold)]
    units += [(0, order) for order in range(fold)]

    def products_between(piece):
        pieces = fold * groups
        mine = units[piece * len(units) // pieces:(piece + 1) * len(units) // pieces]
        if not mine:
            return

        @pl.when(distance < planes - 1)
        def _():
            if mine[0] == units[0]:
                await_rows()
            for unit in mine:
                if unit in units[:fold]:
                    await_columns(unit[1])
                partial_tiles(*unit)

    for step in range(1, planes):
        below, above = plane - step, plane + step
        for order in range(fold):
            chunk = other_part(order)
            for g in range(groups):
                @pl.when(below >= 0)
                def _():
                    z_copy(0, below, chunk, g).wait_recv()

                    @pl.when(plane < planes - 1)
                    def _():
                        z_copy(0, below, chunk, g).start()

                    spread(below, order, g)

                @pl.when(above < planes)
                def _():
                    z_copy(1, above, chunk, g).wait_recv()

                    @pl.when(plane > 0)
                    def _():
                        z_copy(1, above, chunk, g).start()

                    spread(above, order, g)

                if step == planes - 1:
                    products_between(order * groups + g)
                elif step == planes - 2 and order * groups + g == min(1, fold * groups - 1):
                    pass_rows()

    @pl.when(distance == planes - 1)
    def _():
        await_rows()
        for order in range(fold):
            await_columns(order)
            for step in range(1, fold):
                partial_tiles(step, order)
            partial_tiles(0, order)

    prior_fetched.wait()
    for order in range(fold):
        chunk = other_part(order)
        for g in range(groups):
            update = total[part, chunk, g]
            for step in range(1, fold):
                t_copy(step, chunk, g).wait_recv()
                update = update + inbox[step - 1, chunk, g]
            for h in range(groups):
                a, b = row * groups + g, col * block_cols + chunk * groups + h
                kept = pattern_ref[jnp.minimum(a, b), jnp.maximum(a, b)] == 1
                down = pl.ds(pl.multiple_of((chunk * groups + h) * size, size), size)
                across = slice(g * size, (g + 1) * size)
                out_ref[across, down] = prior_ref[across, down] + jnp.where(
                    kept, update[:, h * size:(h + 1) * size], jnp.zeros((size, size), jnp.float32))

    for step in range(1, fold):
        for g in range(groups):
            y_copy(step, g, part).wait_send()
            for chunk in range(fold):
                t_copy(step, chunk, g).wait_send()
    for index in range(planes // 2):
        near_copy(col, index, col).wait_send()
    for step in far_steps:
        far_copy(step, col).wait_send()
    for chunk in range(fold):
        for g in range(groups):
            for step in range(1, planes):
                x_copy(other_col(step), chunk, g, col).wait_send()
            for from_plane in range(planes):
                @pl.when((from_plane <= plane) & (plane < planes - 1))
                def _():
                    z_copy(0, from_plane, chunk, g).wait_send()

                @pl.when((from_plane >= plane) & (plane > 0))
                def _():
                    z_copy(1, from_plane, chunk, g).wait_send()


def on_device(panels, obs_of, counts, inv_var, pattern, prior):
    planes = lax.axis_size("col")
    fold = lax.axis_size("row") // planes
    groups, share, size, _ = panels.shape
    depth = size // fold
    names = -(-inv_var.shape[0] // 128) * 128
    smem = pl.BlockSpec(memory_space=pltpu.SMEM)
    vmem = pl.BlockSpec(memory_space=pltpu.VMEM)
    anywhere = pl.BlockSpec(memory_space=pl.ANY)
    dma = pltpu.SemaphoreType.DMA
    others = max(fold - 1, 1)
    panel = (fold, groups, share, depth, size)
    turned = (fold, groups, size, share * depth)
    tile = (fold, groups, size, groups * size)
    return pl.pallas_call(
        functools.partial(kernel, planes, fold),
        out_shape=jax.ShapeDtypeStruct(prior.shape, prior.dtype),
        in_specs=[smem, smem, smem, vmem, vmem, anywhere, anywhere],
        out_specs=vmem,
        scratch_shapes=[
            pltpu.VMEM(panels.shape, jnp.bfloat16),
            pltpu.VMEM(prior.shape, jnp.float32),
            pltpu.VMEM((obs_of.shape[0], names), jnp.int32),
            pltpu.SMEM((obs_of.shape[0], names), jnp.int32),
            pltpu.VMEM((size, groups * share), jnp.float32),
            pltpu.VMEM((others,) + panel[1:], jnp.bfloat16),
            pltpu.VMEM((planes,) + panel, jnp.bfloat16),
            pltpu.VMEM(turned, jnp.bfloat16),
            pltpu.VMEM((planes,) + turned, jnp.bfloat16),
            (pltpu.VMEM((planes,) + panel[1:], jnp.bfloat16),) * fold,
            pltpu.VMEM((fold,) + tile, jnp.float32),
            pltpu.VMEM((others,) + tile, jnp.float32),
            dma((others, groups)), dma((fold, groups)),
            dma((2, planes, fold, groups)), dma((planes, fold, groups)),
            dma((planes, fold, groups)), dma((planes, fold, groups)),
            dma((planes,)), dma((planes,)),
            dma((planes // 2,)), dma((planes // 2,)),
            dma((others, fold, groups)), dma((others, fold, groups)),
            dma((fold, groups)), dma, dma, dma,
        ],
        compiler_params=pltpu.CompilerParams(
            collective_id=0, has_side_effects=True, vmem_limit_bytes=60 * 1024 * 1024),
    )(obs_of, counts, pattern, obs_of, inv_var, panels, prior)


def solution(mesh):
    placed = (P("row", "col", None, None), P(), P(), P(), P(), P("row", "col"))
    return jax.shard_map(
        on_device, mesh=mesh, in_specs=placed, out_specs=P("row", "col"), check_vma=False
    )
```

```python
import functools

import jax
import jax.numpy as jnp
from jax import lax
from jax.experimental import pallas as pl
from jax.experimental.pallas import tpu as pltpu
from jax.sharding import PartitionSpec as P

MESH = pl.DeviceIdType.MESH


def kernel(planes, fold, obs_ref, counts_ref, pattern_ref, ids_ref, var_ref, source_ref, prior_source, out_ref,
           panels_ref, prior_ref, table, place_ref, weights, leaving, held, turned, rows, cols, total, inbox,
           y_send, y_recv, z_send, z_recv, x_send, x_recv, r_send, r_recv, n_send, n_recv,
           t_send, t_recv, keep, fetch, prior_fetch, place_fetch):
    row, col = lax.axis_index("row"), lax.axis_index("col")
    plane, part = row // fold, row % fold
    groups, share, size = panels_ref.shape[0], panels_ref.shape[1], panels_ref.shape[2]
    depth = size // fold
    wide = share * depth
    slot_count = ids_ref.shape[1]
    near = col + 1 - 2 * lax.rem(col, 2)
    far_steps = range(2, planes, 2)

    def at(other_row, other_col):
        return {"row": other_row, "col": other_col}

    def other_plane(step):
        return lax.rem(plane + step, planes)

    def other_col(step):
        return lax.rem(col + step, planes)

    def other_part(step):
        return lax.rem(part + step, fold)

    fetched = pltpu.make_async_copy(source_ref, panels_ref, fetch)
    fetched.start()
    prior_fetched = pltpu.make_async_copy(prior_source, prior_ref, prior_fetch)
    prior_fetched.start()
    partners = [at(other_plane(s) * fold + part, col) for s in (1, planes - 1)]
    partners += [at(row, other_col(s)) for s in range(1, planes)]
    partners += [at(plane * fold + other_part(s), col) for s in range(1, fold)]
    barrier = pltpu.get_barrier_semaphore()
    for partner in partners:
        pl.semaphore_signal(barrier, inc=1, device_id=partner, device_id_type=MESH)

    factors = []
    for g in range(groups):
        block = row * groups + g
        for p in range(share):
            slot = col * share + p
            live = jnp.where(slot < counts_ref[block], 1.0, 0.0)
            factors.append(jnp.sqrt(var_ref[pl.ds(obs_ref[block, slot], 1), :]) * live)
    weights[...] = jnp.concatenate(factors, axis=0).T
    fetched.wait()

    def scaled(to_part, g, p):
        j = g * share + p
        lines = pl.ds(pl.multiple_of(to_part * depth, depth), depth)
        value = panels_ref[g, p, lines, :].astype(jnp.float32) * weights[lines, j:j + 1]
        return value.astype(jnp.bfloat16)

    def copy(src, dst, send, recv, device):
        return pltpu.make_async_remote_copy(
            src_ref=src, dst_ref=dst, send_sem=send, recv_sem=recv,
            device_id=device, device_id_type=MESH)

    def y_copy(step, g, landing):
        return copy(leaving.at[step - 1, g], held.at[plane, landing, g], y_send.at[step - 1, g],
                    y_recv.at[landing, g], at(plane * fold + other_part(step), col))

    def z_copy(way, from_plane, chunk, g):
        target = lax.rem(plane + (1 if way == 0 else planes - 1), planes)
        return copy(held.at[from_plane, chunk, g], held.at[from_plane, chunk, g],
                    z_send.at[way, from_plane, chunk, g], z_recv.at[from_plane, chunk, g],
                    at(target * fold + part, col))

    def slots_of(slot_col):
        return pl.ds(slot_col * share, share)

    def x_copy(to_col, order, g, landing):
        return copy(held.at[to_col, other_part(order), g], cols[order].at[g, slots_of(landing)],
                    x_send.at[to_col, order, g], x_recv.at[landing, order, g], at(row, to_col))

    def keep_copy(order, g):
        return pltpu.make_async_copy(held.at[col, other_part(order), g], cols[order].at[g, slots_of(col)],
                                     keep.at[order, g])

    def far_copy(step, landing):
        return copy(turned, rows.at[landing], r_send.at[step], r_recv.at[landing], at(row, other_col(step)))

    def near_copy(slot, index, landing):
        source = turned if index == 0 else rows.at[slot]
        return copy(source, rows.at[landing], n_send.at[index], n_recv.at[index], at(row, near))

    def t_copy(step, chunk, g):
        return copy(total.at[other_part(step), chunk, g], inbox.at[step - 1, chunk, g],
                    t_send.at[step - 1, chunk, g], t_recv.at[step - 1, chunk, g],
                    at(plane * fold + other_part(step), col))

    def spread(from_plane, order, g):
        @pl.when(from_plane != col)
        def _():
            x_copy(from_plane, order, g, col).start()

        @pl.when(from_plane == col)
        def _():
            keep_copy(order, g).start()

    def begin(chunk, g):
        @pl.when(plane < planes - 1)
        def _():
            z_copy(0, plane, chunk, g).start()

        @pl.when(plane > 0)
        def _():
            z_copy(1, plane, chunk, g).start()

    def turn(chunk, g):
        turned[chunk, g] = held[plane, chunk, g].reshape(wide, size).T

    for step in range(1, fold):
        for g in range(groups):
            for p in range(share):
                leaving[step - 1, g, p] = scaled(other_part(step), g, p)
    pl.semaphore_wait(barrier, len(partners))
    for step in range(1, fold):
        for g in range(groups):
            y_copy(step, g, part).start()
    for g in range(groups):
        for p in range(share):
            held[plane, part, g, p] = scaled(part, g, p)
        begin(part, g)
    for g in range(groups):
        spread(plane, 0, g)
        turn(part, g)
    for step in range(1, fold):
        for g in range(groups):
            y_copy(step, g, other_part(step)).wait_recv()
            begin(other_part(step), g)
        for g in range(groups):
            spread(plane, step, g)
            turn(other_part(step), g)
    ids = lax.broadcasted_iota(jnp.int32, table.shape, 1)
    found = jnp.full(table.shape, slot_count, jnp.int32)
    for p in range(slot_count):
        found = jnp.where(ids_ref[:, p:p + 1] == ids, p, found)
    table[...] = found
    placed = pltpu.make_async_copy(table, place_ref, place_fetch)
    placed.start()
    for order in range(fold):
        for h in range(groups):
            cols[order][h, slot_count] = jnp.zeros((depth, size), jnp.bfloat16)
    own_row = pltpu.make_async_copy(turned, rows.at[col], fetch)
    own_row.start()
    near_copy(col, 0, col).start()
    for step in far_steps:
        far_copy(step, col).start()

    def pass_rows():
        for index, step in enumerate(far_steps):
            slot = other_col(step)
            far_copy(step, slot).wait_recv()
            near_copy(slot, index + 1, slot).start()

    block_cols = groups * fold
    paired = 2 if planes % 2 == 0 else 1

    def partial_tiles(step_part, order):
        row_part, chunk = other_part(step_part), other_part(order)
        first = col * block_cols + chunk * groups
        for g in range(groups):
            a = (plane * fold + row_part) * groups + g

            def step(i, unused):
                for slot_col in [i * paired + k for k in range(paired)]:
                    lines = []
                    for p in range(share):
                        obs = obs_ref[a, slot_col * share + p]
                        lines.append(jnp.concatenate(
                            [cols[order][h, place_ref[first + h, obs]] for h in range(groups)], axis=1))
                    total[row_part, chunk, g] += jnp.dot(
                        rows[slot_col, row_part, g], jnp.concatenate(lines, axis=0),
                        preferred_element_type=jnp.float32)
                return unused

            total[row_part, chunk, g] = jnp.zeros(total.shape[3:], jnp.float32)
            lax.fori_loop(0, planes // paired, step, 0)
            if step_part > 0:
                t_copy(step_part, chunk, g).start()

    def await_rows():
        placed.wait()
        own_row.wait()
        near_copy(near, 0, near).wait_recv()
        for index, step in enumerate(far_steps):
            slot = lax.rem(near + step, planes)
            near_copy(slot, index + 1, slot).wait_recv()

    def await_columns(order):
        for g in range(groups):
            keep_copy(order, g).wait()
            for step in range(1, planes):
                x_copy(col, order, g, other_col(step)).wait_recv()

    distance = jnp.maximum(plane - col, col - plane)
    units = [(step, order) for step in range(1, fold) for order in range(fold)]
    units += [(0, order) for order in range(fold)]

    def products_between(piece):
        pieces = fold * groups
        mine = units[piece * len(units) // pieces:(piece + 1) * len(units) // pieces]
        if not mine:
            return

        @pl.when(distance < planes - 1)
        def _():
            if mine[0] == units[0]:
                await_rows()
            for unit in mine:
                if unit in units[:fold]:
                    await_columns(unit[1])
                partial_tiles(*unit)

    for step in range(1, planes):
        below, above = plane - step, plane + step
        for order in range(fold):
            chunk = other_part(order)
            for g in range(groups):
                @pl.when(below >= 0)
                def _():
                    z_copy(0, below, chunk, g).wait_recv()

                    @pl.when(plane < planes - 1)
                    def _():
                        z_copy(0, below, chunk, g).start()

                    spread(below, order, g)

                @pl.when(above < planes)
                def _():
                    z_copy(1, above, chunk, g).wait_recv()

                    @pl.when(plane > 0)
                    def _():
                        z_copy(1, above, chunk, g).start()

                    spread(above, order, g)

                if step == planes - 1:
                    products_between(order * groups + g)
                elif step == planes - 2 and order * groups + g == min(1, fold * groups - 1):
                    pass_rows()

    @pl.when(distance == planes - 1)
    def _():
        await_rows()
        for order in range(fold):
            await_columns(order)
            for step in range(1, fold):
                partial_tiles(step, order)
            partial_tiles(0, order)

    prior_fetched.wait()
    for order in range(fold):
        chunk = other_part(order)
        for g in range(groups):
            update = total[part, chunk, g]
            for step in range(1, fold):
                t_copy(step, chunk, g).wait_recv()
                update = update + inbox[step - 1, chunk, g]
            for h in range(groups):
                a, b = row * groups + g, col * block_cols + chunk * groups + h
                kept = pattern_ref[jnp.minimum(a, b), jnp.maximum(a, b)] == 1
                down = pl.ds(pl.multiple_of((chunk * groups + h) * size, size), size)
                across = slice(g * size, (g + 1) * size)
                out_ref[across, down] = prior_ref[across, down] + jnp.where(
                    kept, update[:, h * size:(h + 1) * size], jnp.zeros((size, size), jnp.float32))

    for step in range(1, fold):
        for g in range(groups):
            y_copy(step, g, part).wait_send()
            for chunk in range(fold):
                t_copy(step, chunk, g).wait_send()
    for index in range(planes // 2):
        near_copy(col, index, col).wait_send()
    for step in far_steps:
        far_copy(step, col).wait_send()
    for chunk in range(fold):
        for g in range(groups):
            for step in range(1, planes):
                x_copy(other_col(step), chunk, g, col).wait_send()
            for from_plane in range(planes):
                @pl.when((from_plane <= plane) & (plane < planes - 1))
                def _():
                    z_copy(0, from_plane, chunk, g).wait_send()

                @pl.when((from_plane >= plane) & (plane > 0))
                def _():
                    z_copy(1, from_plane, chunk, g).wait_send()


def on_device(panels, obs_of, counts, inv_var, pattern, prior):
    planes = lax.axis_size("col")
    fold = lax.axis_size("row") // planes
    groups, share, size, _ = panels.shape
    depth = size // fold
    names = -(-inv_var.shape[0] // 128) * 128
    smem = pl.BlockSpec(memory_space=pltpu.SMEM)
    vmem = pl.BlockSpec(memory_space=pltpu.VMEM)
    anywhere = pl.BlockSpec(memory_space=pl.ANY)
    dma = pltpu.SemaphoreType.DMA
    others = max(fold - 1, 1)
    panel = (fold, groups, share, depth, size)
    turned = (fold, groups, size, share * depth)
    tile = (fold, groups, size, groups * size)
    return pl.pallas_call(
        functools.partial(kernel, planes, fold),
        out_shape=jax.ShapeDtypeStruct(prior.shape, prior.dtype),
        in_specs=[smem, smem, smem, vmem, vmem, anywhere, anywhere],
        out_specs=vmem,
        scratch_shapes=[
            pltpu.VMEM(panels.shape, jnp.bfloat16),
            pltpu.VMEM(prior.shape, jnp.float32),
            pltpu.VMEM((obs_of.shape[0], names), jnp.int32),
            pltpu.SMEM((obs_of.shape[0], names), jnp.int32),
            pltpu.VMEM((size, groups * share), jnp.float32),
            pltpu.VMEM((others,) + panel[1:], jnp.bfloat16),
            pltpu.VMEM((planes,) + panel, jnp.bfloat16),
            pltpu.VMEM(turned, jnp.bfloat16),
            pltpu.VMEM((planes,) + turned, jnp.bfloat16),
            (pltpu.VMEM((groups, obs_of.shape[1] + 1, depth, size), jnp.bfloat16),) * fold,
            pltpu.VMEM((fold,) + tile, jnp.float32),
            pltpu.VMEM((others,) + tile, jnp.float32),
            dma((others, groups)), dma((fold, groups)),
            dma((2, planes, fold, groups)), dma((planes, fold, groups)),
            dma((planes, fold, groups)), dma((planes, fold, groups)),
            dma((planes,)), dma((planes,)),
            dma((planes // 2,)), dma((planes // 2,)),
            dma((others, fold, groups)), dma((others, fold, groups)),
            dma((fold, groups)), dma, dma, dma,
        ],
        compiler_params=pltpu.CompilerParams(
            collective_id=0, has_side_effects=True, vmem_limit_bytes=60 * 1024 * 1024),
    )(obs_of, counts, pattern, obs_of, inv_var, panels, prior)


def solution(mesh):
    placed = (P("row", "col", None, None), P(), P(), P(), P(), P("row", "col"))
    return jax.shard_map(
        on_device, mesh=mesh, in_specs=placed, out_specs=P("row", "col"), check_vma=False
    )
```

```python
import functools

import jax
import jax.numpy as jnp
from jax import lax
from jax.experimental import pallas as pl
from jax.experimental.pallas import tpu as pltpu
from jax.sharding import PartitionSpec as P

MESH = pl.DeviceIdType.MESH


def kernel(planes, fold, source_ref, obs_source, counts_source, var_source, pattern_source, prior_source, out_ref,
           obs_ref, counts_ref, pattern_ref, ids_ref, var_ref, panels_ref, prior_ref, table, place_ref, weights, leaving, held, turned, rows, cols, total, inbox,
           y_send, y_recv, z_send, z_recv, x_send, x_recv, r_send, r_recv, n_send, n_recv,
           t_send, t_recv, keep, fetch, place_fetch):
    row, col = lax.axis_index("row"), lax.axis_index("col")
    plane, part = row // fold, row % fold
    groups, share, size = panels_ref.shape[0], panels_ref.shape[1], panels_ref.shape[2]
    depth = size // fold
    wide = share * depth
    slot_count = ids_ref.shape[1]
    near = col + 1 - 2 * lax.rem(col, 2)
    far_steps = range(2, planes, 2)

    def at(other_row, other_col):
        return {"row": other_row, "col": other_col}

    def other_plane(step):
        return lax.rem(plane + step, planes)

    def other_col(step):
        return lax.rem(col + step, planes)

    def other_part(step):
        return lax.rem(part + step, fold)

    fetches = [pltpu.make_async_copy(source, target, fetch.at[index]) for index, (source, target) in enumerate((
        (obs_source, obs_ref), (counts_source, counts_ref), (var_source, var_ref), (source_ref, panels_ref),
        (obs_source, ids_ref), (pattern_source, pattern_ref), (prior_source, prior_ref)))]
    for fetched in fetches:
        fetched.start()
    partners = [at(other_plane(s) * fold + part, col) for s in (1, planes - 1)]
    partners += [at(row, other_col(s)) for s in range(1, planes)]
    partners += [at(plane * fold + other_part(s), col) for s in range(1, fold)]
    barrier = pltpu.get_barrier_semaphore()
    for partner in partners:
        pl.semaphore_signal(barrier, inc=1, device_id=partner, device_id_type=MESH)

    for fetched in fetches[:3]:
        fetched.wait()
    factors = []
    for g in range(groups):
        block = row * groups + g
        for p in range(share):
            slot = col * share + p
            live = jnp.where(slot < counts_ref[block], 1.0, 0.0)
            factors.append(jnp.sqrt(var_ref[pl.ds(obs_ref[block, slot], 1), :]) * live)
    weights[...] = jnp.concatenate(factors, axis=0).T
    fetches[3].wait()

    def scaled(to_part, g, p):
        j = g * share + p
        lines = pl.ds(pl.multiple_of(to_part * depth, depth), depth)
        value = panels_ref[g, p, lines, :].astype(jnp.float32) * weights[lines, j:j + 1]
        return value.astype(jnp.bfloat16)

    def copy(src, dst, send, recv, device):
        return pltpu.make_async_remote_copy(
            src_ref=src, dst_ref=dst, send_sem=send, recv_sem=recv,
            device_id=device, device_id_type=MESH)

    def y_copy(step, g, landing):
        return copy(leaving.at[step - 1, g], held.at[plane, landing, g], y_send.at[step - 1, g],
                    y_recv.at[landing, g], at(plane * fold + other_part(step), col))

    def z_copy(way, from_plane, chunk, g):
        target = lax.rem(plane + (1 if way == 0 else planes - 1), planes)
        return copy(held.at[from_plane, chunk, g], held.at[from_plane, chunk, g],
                    z_send.at[way, from_plane, chunk, g], z_recv.at[from_plane, chunk, g],
                    at(target * fold + part, col))

    def slots_of(slot_col):
        return pl.ds(slot_col * share, share)

    def x_copy(to_col, order, g, landing):
        return copy(held.at[to_col, other_part(order), g], cols[order * groups + g].at[slots_of(landing)],
                    x_send.at[to_col, order, g], x_recv.at[landing, order, g], at(row, to_col))

    def keep_copy(order, g):
        return pltpu.make_async_copy(held.at[col, other_part(order), g], cols[order * groups + g].at[slots_of(col)],
                                     keep.at[order, g])

    def far_copy(step, landing):
        return copy(turned, rows.at[landing], r_send.at[step], r_recv.at[landing], at(row, other_col(step)))

    def near_copy(slot, index, landing):
        source = turned if index == 0 else rows.at[slot]
        return copy(source, rows.at[landing], n_send.at[index], n_recv.at[index], at(row, near))

    def t_copy(step, chunk, h, g):
        return copy(total.at[other_part(step), chunk, h, g], inbox.at[step - 1, chunk, h, g],
                    t_send.at[step - 1, chunk, h, g], t_recv.at[step - 1, chunk, h, g],
                    at(plane * fold + other_part(step), col))

    def spread(from_plane, order, g):
        @pl.when(from_plane != col)
        def _():
            x_copy(from_plane, order, g, col).start()

        @pl.when(from_plane == col)
        def _():
            keep_copy(order, g).start()

    def begin(chunk, g):
        @pl.when(plane < planes - 1)
        def _():
            z_copy(0, plane, chunk, g).start()

        @pl.when(plane > 0)
        def _():
            z_copy(1, plane, chunk, g).start()

    def turn(chunk, g):
        turned[chunk, g] = held[plane, chunk, g].reshape(wide, size).T

    for step in range(1, fold):
        for g in range(groups):
            for p in range(share):
                leaving[step - 1, g, p] = scaled(other_part(step), g, p)
    pl.semaphore_wait(barrier, len(partners))
    for step in range(1, fold):
        for g in range(groups):
            y_copy(step, g, part).start()
    for g in range(groups):
        for p in range(share):
            held[plane, part, g, p] = scaled(part, g, p)
        begin(part, g)
    for g in range(groups):
        spread(plane, 0, g)
        turn(part, g)
    for step in range(1, fold):
        for g in range(groups):
            y_copy(step, g, other_part(step)).wait_recv()
            begin(other_part(step), g)
        for g in range(groups):
            spread(plane, step, g)
            turn(other_part(step), g)
    ids = lax.broadcasted_iota(jnp.int32, table.shape, 1)
    fetches[4].wait()
    found = jnp.full(table.shape, slot_count, jnp.int32)
    for p in range(slot_count):
        found = jnp.where(ids_ref[:, p:p + 1] == ids, p, found)
    table[...] = found
    placed = pltpu.make_async_copy(table, place_ref, place_fetch)
    placed.start()
    for piece in range(fold * groups):
        cols[piece][slot_count] = jnp.zeros((depth, size), jnp.bfloat16)
    own_row = pltpu.make_async_copy(turned, rows.at[col], fetch.at[len(fetches)])
    own_row.start()
    near_copy(col, 0, col).start()
    for step in far_steps:
        far_copy(step, col).start()

    def pass_rows():
        for index, step in enumerate(far_steps):
            slot = other_col(step)
            far_copy(step, slot).wait_recv()
            near_copy(slot, index + 1, slot).start()

    block_cols = groups * fold
    paired = 2 if planes % 2 == 0 else 1

    def partial_tiles(step_part, piece):
        row_part, chunk, h = other_part(step_part), other_part(piece // groups), piece % groups
        b = col * block_cols + chunk * groups + h

        def step(i, unused):
            for slot_col in [i * paired + k for k in range(paired)]:
                for g in range(groups):
                    a = (plane * fold + row_part) * groups + g
                    lines = [cols[piece][place_ref[b, obs_ref[a, slot_col * share + p]]] for p in range(share)]
                    total[row_part, chunk, h, g] += jnp.dot(
                        rows[slot_col, row_part, g], jnp.concatenate(lines, axis=0),
                        preferred_element_type=jnp.float32)
            return unused

        total[row_part, chunk, h] = jnp.zeros(total.shape[3:], jnp.float32)
        lax.fori_loop(0, planes // paired, step, 0)
        if step_part > 0:
            for g in range(groups):
                t_copy(step_part, chunk, h, g).start()

    def await_rows():
        placed.wait()
        own_row.wait()
        near_copy(near, 0, near).wait_recv()
        for index, step in enumerate(far_steps):
            slot = lax.rem(near + step, planes)
            near_copy(slot, index + 1, slot).wait_recv()

    def await_columns(piece):
        order, g = piece // groups, piece % groups
        keep_copy(order, g).wait()
        for step in range(1, planes):
            x_copy(col, order, g, other_col(step)).wait_recv()

    distance = jnp.maximum(plane - col, col - plane)
    pieces = fold * groups
    units = [(step, piece) for step in range(1, fold) for piece in range(pieces)]
    units += [(0, piece) for piece in range(pieces)]

    def products_between(turn_at):
        mine = units[turn_at * len(units) // pieces:(turn_at + 1) * len(units) // pieces]

        @pl.when(distance < planes - 1)
        def _():
            if turn_at == 0:
                await_rows()
            for unit in mine:
                if unit in units[:pieces]:
                    await_columns(unit[1])
                partial_tiles(*unit)

    for step in range(1, planes):
        below, above = plane - step, plane + step
        for order in range(fold):
            chunk = other_part(order)
            for g in range(groups):
                @pl.when(below >= 0)
                def _():
                    z_copy(0, below, chunk, g).wait_recv()

                    @pl.when(plane < planes - 1)
                    def _():
                        z_copy(0, below, chunk, g).start()

                    spread(below, order, g)

                @pl.when(above < planes)
                def _():
                    z_copy(1, above, chunk, g).wait_recv()

                    @pl.when(plane > 0)
                    def _():
                        z_copy(1, above, chunk, g).start()

                    spread(above, order, g)

                if step == planes - 1:
                    products_between(order * groups + g)
                elif step == planes - 2 and order * groups + g == min(1, fold * groups - 1):
                    pass_rows()

    @pl.when(distance == planes - 1)
    def _():
        await_rows()
        for piece in range(pieces):
            await_columns(piece)
            for step in range(1, fold):
                partial_tiles(step, piece)
            partial_tiles(0, piece)

    for fetched in fetches[5:]:
        fetched.wait()
    for piece in range(pieces):
        chunk, h = other_part(piece // groups), piece % groups
        for g in range(groups):
            update = total[part, chunk, h, g]
            for step in range(1, fold):
                t_copy(step, chunk, h, g).wait_recv()
                update = update + inbox[step - 1, chunk, h, g]
            a, b = row * groups + g, col * block_cols + chunk * groups + h
            kept = pattern_ref[jnp.minimum(a, b), jnp.maximum(a, b)] == 1
            across = slice(g * size, (g + 1) * size)
            down = pl.ds(pl.multiple_of((chunk * groups + h) * size, size), size)
            out_ref[across, down] = prior_ref[across, down] + jnp.where(kept, update, jnp.zeros_like(update))

    for step in range(1, fold):
        for g in range(groups):
            y_copy(step, g, part).wait_send()
            for chunk in range(fold):
                for h in range(groups):
                    t_copy(step, chunk, h, g).wait_send()
    for index in range(planes // 2):
        near_copy(col, index, col).wait_send()
    for step in far_steps:
        far_copy(step, col).wait_send()
    for chunk in range(fold):
        for g in range(groups):
            for step in range(1, planes):
                x_copy(other_col(step), chunk, g, col).wait_send()
            for from_plane in range(planes):
                @pl.when((from_plane <= plane) & (plane < planes - 1))
                def _():
                    z_copy(0, from_plane, chunk, g).wait_send()

                @pl.when((from_plane >= plane) & (plane > 0))
                def _():
                    z_copy(1, from_plane, chunk, g).wait_send()


def on_device(panels, obs_of, counts, inv_var, pattern, prior):
    planes = lax.axis_size("col")
    fold = lax.axis_size("row") // planes
    groups, share, size, _ = panels.shape
    depth = size // fold
    names = -(-inv_var.shape[0] // 128) * 128
    far_memory = pl.BlockSpec(memory_space=pltpu.HBM)
    dma = pltpu.SemaphoreType.DMA
    others = max(fold - 1, 1)
    panel = (fold, groups, share, depth, size)
    turned = (fold, groups, size, share * depth)
    tile = (fold, groups, groups, size, size)
    return pl.pallas_call(
        functools.partial(kernel, planes, fold),
        out_shape=jax.ShapeDtypeStruct(prior.shape, prior.dtype),
        in_specs=[far_memory] * 6,
        out_specs=pl.BlockSpec(memory_space=pltpu.VMEM),
        scratch_shapes=[
            pltpu.SMEM(obs_of.shape, jnp.int32),
            pltpu.SMEM(counts.shape, jnp.int32),
            pltpu.SMEM(pattern.shape, jnp.int32),
            pltpu.VMEM(obs_of.shape, jnp.int32),
            pltpu.VMEM(inv_var.shape, jnp.float32),
            pltpu.VMEM(panels.shape, jnp.bfloat16),
            pltpu.VMEM(prior.shape, jnp.float32),
            pltpu.VMEM((obs_of.shape[0], names), jnp.int32),
            pltpu.SMEM((obs_of.shape[0], names), jnp.int32),
            pltpu.VMEM((size, groups * share), jnp.float32),
            pltpu.VMEM((others,) + panel[1:], jnp.bfloat16),
            pltpu.VMEM((planes,) + panel, jnp.bfloat16),
            pltpu.VMEM(turned, jnp.bfloat16),
            pltpu.VMEM((planes,) + turned, jnp.bfloat16),
            (pltpu.VMEM((obs_of.shape[1] + 1, depth, size), jnp.bfloat16),) * (fold * groups),
            pltpu.VMEM((fold,) + tile, jnp.float32),
            pltpu.VMEM((others,) + tile, jnp.float32),
            dma((others, groups)), dma((fold, groups)),
            dma((2, planes, fold, groups)), dma((planes, fold, groups)),
            dma((planes, fold, groups)), dma((planes, fold, groups)),
            dma((planes,)), dma((planes,)),
            dma((planes // 2,)), dma((planes // 2,)),
            dma((others, fold, groups, groups)), dma((others, fold, groups, groups)),
            dma((fold, groups)), dma((8,)), dma,
        ],
        compiler_params=pltpu.CompilerParams(
            collective_id=0, has_side_effects=True, vmem_limit_bytes=60 * 1024 * 1024),
    )(panels, obs_of, counts, inv_var, pattern, prior)


def solution(mesh):
    placed = (P("row", "col", None, None), P(), P(), P(), P(), P("row", "col"))
    return jax.shard_map(
        on_device, mesh=mesh, in_specs=placed, out_specs=P("row", "col"), check_vma=False
    )
```

```python
import functools

import jax
import jax.numpy as jnp
from jax import lax
from jax.experimental import pallas as pl
from jax.experimental.pallas import tpu as pltpu
from jax.sharding import PartitionSpec as P

MESH = pl.DeviceIdType.MESH


def kernel(planes, fold, source_ref, obs_source, counts_source, var_source, pattern_source, prior_source, out_ref,
           obs_ref, counts_ref, pattern_ref, ids_ref, var_ref, panels_ref, prior_ref, table, place_ref, weights, leaving, held, turned, rows, cols, total, inbox,
           y_send, y_recv, z_send, z_recv, x_send, x_recv, r_send, r_recv, n_send, n_recv,
           t_send, t_recv, keep, fetch, place_fetch):
    row, col = lax.axis_index("row"), lax.axis_index("col")
    plane, part = row // fold, row % fold
    groups, share, size = panels_ref.shape[0], panels_ref.shape[1], panels_ref.shape[2]
    depth = size // fold
    wide = share * depth
    slot_count = ids_ref.shape[1]
    near = col + 1 - 2 * lax.rem(col, 2)
    far_steps = range(2, planes, 2)

    def at(other_row, other_col):
        return {"row": other_row, "col": other_col}

    def other_plane(step):
        return lax.rem(plane + step, planes)

    def other_col(step):
        return lax.rem(col + step, planes)

    def other_part(step):
        return lax.rem(part + step, fold)

    fetches = [pltpu.make_async_copy(source, target, fetch.at[index]) for index, (source, target) in enumerate((
        (obs_source, obs_ref), (counts_source, counts_ref), (var_source, var_ref), (source_ref, panels_ref),
        (obs_source, ids_ref), (pattern_source, pattern_ref), (prior_source, prior_ref)))]
    for fetched in fetches:
        fetched.start()
    partners = [at(other_plane(s) * fold + part, col) for s in (1, planes - 1)]
    partners += [at(row, other_col(s)) for s in range(1, planes)]
    partners += [at(plane * fold + other_part(s), col) for s in range(1, fold)]
    barrier = pltpu.get_barrier_semaphore()
    for partner in partners:
        pl.semaphore_signal(barrier, inc=1, device_id=partner, device_id_type=MESH)

    for fetched in fetches[:3]:
        fetched.wait()
    factors = []
    for g in range(groups):
        block = row * groups + g
        for p in range(share):
            slot = col * share + p
            live = jnp.where(slot < counts_ref[block], 1.0, 0.0)
            factors.append(jnp.sqrt(var_ref[pl.ds(obs_ref[block, slot], 1), :]) * live)
    weights[...] = jnp.concatenate(factors, axis=0).T
    fetches[3].wait()

    def scaled(to_part, g, p):
        j = g * share + p
        lines = pl.ds(pl.multiple_of(to_part * depth, depth), depth)
        value = panels_ref[g, p, lines, :].astype(jnp.float32) * weights[lines, j:j + 1]
        return value.astype(jnp.bfloat16)

    def copy(src, dst, send, recv, device):
        return pltpu.make_async_remote_copy(
            src_ref=src, dst_ref=dst, send_sem=send, recv_sem=recv,
            device_id=device, device_id_type=MESH)

    def y_copy(step, g, landing):
        return copy(leaving.at[step - 1, g], held.at[plane, landing, g], y_send.at[step - 1, g],
                    y_recv.at[landing, g], at(plane * fold + other_part(step), col))

    def z_copy(way, from_plane, chunk, g):
        target = lax.rem(plane + (1 if way == 0 else planes - 1), planes)
        return copy(held.at[from_plane, chunk, g], held.at[from_plane, chunk, g],
                    z_send.at[way, from_plane, chunk, g], z_recv.at[from_plane, chunk, g],
                    at(target * fold + part, col))

    def slots_of(slot_col):
        return pl.ds(slot_col * share, share)

    def x_copy(to_col, order, g, landing):
        return copy(held.at[to_col, other_part(order), g], cols[order * groups + g].at[slots_of(landing)],
                    x_send.at[to_col, order, g], x_recv.at[landing, order, g], at(row, to_col))

    def keep_copy(order, g):
        return pltpu.make_async_copy(held.at[col, other_part(order), g], cols[order * groups + g].at[slots_of(col)],
                                     keep.at[order, g])

    def far_copy(step, chunk, landing):
        return copy(turned.at[chunk], rows.at[landing, chunk], r_send.at[step, chunk],
                    r_recv.at[landing, chunk], at(row, other_col(step)))

    def near_copy(slot, index, landing):
        source = turned if index == 0 else rows.at[slot]
        return copy(source, rows.at[landing], n_send.at[index], n_recv.at[index], at(row, near))

    def t_copy(step, chunk, h, g):
        return copy(total.at[other_part(step), chunk, h, g], inbox.at[step - 1, chunk, h, g],
                    t_send.at[step - 1, chunk, h, g], t_recv.at[step - 1, chunk, h, g],
                    at(plane * fold + other_part(step), col))

    def spread(from_plane, order, g):
        @pl.when(from_plane != col)
        def _():
            x_copy(from_plane, order, g, col).start()

        @pl.when(from_plane == col)
        def _():
            keep_copy(order, g).start()

    def begin(chunk, g):
        @pl.when(plane < planes - 1)
        def _():
            z_copy(0, plane, chunk, g).start()

        @pl.when(plane > 0)
        def _():
            z_copy(1, plane, chunk, g).start()

    def turn(chunk, g):
        turned[chunk, g] = held[plane, chunk, g].reshape(wide, size).T

    for step in range(1, fold):
        for g in range(groups):
            for p in range(share):
                leaving[step - 1, g, p] = scaled(other_part(step), g, p)
    pl.semaphore_wait(barrier, len(partners))
    for step in range(1, fold):
        for g in range(groups):
            y_copy(step, g, part).start()
    for g in range(groups):
        for p in range(share):
            held[plane, part, g, p] = scaled(part, g, p)
        begin(part, g)
    for g in range(groups):
        spread(plane, 0, g)
        turn(part, g)
    for step in far_steps:
        far_copy(step, part, col).start()
    for step in range(1, fold):
        for g in range(groups):
            y_copy(step, g, other_part(step)).wait_recv()
            begin(other_part(step), g)
        for g in range(groups):
            spread(plane, step, g)
            turn(other_part(step), g)
        for far in far_steps:
            far_copy(far, other_part(step), col).start()
    ids = lax.broadcasted_iota(jnp.int32, table.shape, 1)
    fetches[4].wait()
    found = jnp.full(table.shape, slot_count, jnp.int32)
    for p in range(slot_count):
        found = jnp.where(ids_ref[:, p:p + 1] == ids, p, found)
    table[...] = found
    placed = pltpu.make_async_copy(table, place_ref, place_fetch)
    placed.start()
    for piece in range(fold * groups):
        cols[piece][slot_count] = jnp.zeros((depth, size), jnp.bfloat16)
    own_row = pltpu.make_async_copy(turned, rows.at[col], fetch.at[len(fetches)])
    own_row.start()
    near_copy(col, 0, col).start()

    def pass_rows():
        for index, step in enumerate(far_steps):
            slot = other_col(step)
            for chunk in range(fold):
                far_copy(step, chunk, slot).wait_recv()
            near_copy(slot, index + 1, slot).start()

    block_cols = groups * fold
    paired = 2 if planes % 2 == 0 else 1

    def partial_tiles(step_part, piece):
        row_part, chunk, h = other_part(step_part), other_part(piece // groups), piece % groups
        b = col * block_cols + chunk * groups + h

        def step(i, unused):
            for slot_col in [i * paired + k for k in range(paired)]:
                for g in range(groups):
                    a = (plane * fold + row_part) * groups + g
                    lines = [cols[piece][place_ref[b, obs_ref[a, slot_col * share + p]]] for p in range(share)]
                    total[row_part, chunk, h, g] += jnp.dot(
                        rows[slot_col, row_part, g], jnp.concatenate(lines, axis=0),
                        preferred_element_type=jnp.float32)
            return unused

        total[row_part, chunk, h] = jnp.zeros(total.shape[3:], jnp.float32)
        lax.fori_loop(0, planes // paired, step, 0)
        if step_part > 0:
            for g in range(groups):
                t_copy(step_part, chunk, h, g).start()

    def await_rows():
        placed.wait()
        own_row.wait()
        near_copy(near, 0, near).wait_recv()
        for index, step in enumerate(far_steps):
            slot = lax.rem(near + step, planes)
            near_copy(slot, index + 1, slot).wait_recv()

    def await_columns(piece):
        order, g = piece // groups, piece % groups
        keep_copy(order, g).wait()
        for step in range(1, planes):
            x_copy(col, order, g, other_col(step)).wait_recv()

    distance = jnp.maximum(plane - col, col - plane)
    pieces = fold * groups

    def products(piece):
        if piece == 0:
            await_rows()
        await_columns(piece)
        for step_part in range(1, fold):
            partial_tiles(step_part, piece)
        partial_tiles(0, piece)

    def products_between(piece):
        @pl.when(distance < planes - 1)
        def _():
            products(piece)

        if piece > 0:
            @pl.when(distance == planes - 1)
            def _():
                products(piece - 1)

    for step in range(1, planes):
        below, above = plane - step, plane + step
        for order in range(fold):
            chunk = other_part(order)
            for g in range(groups):
                @pl.when(below >= 0)
                def _():
                    z_copy(0, below, chunk, g).wait_recv()

                    @pl.when(plane < planes - 1)
                    def _():
                        z_copy(0, below, chunk, g).start()

                    spread(below, order, g)

                @pl.when(above < planes)
                def _():
                    z_copy(1, above, chunk, g).wait_recv()

                    @pl.when(plane > 0)
                    def _():
                        z_copy(1, above, chunk, g).start()

                    spread(above, order, g)

                if step == planes - 1:
                    products_between(order * groups + g)
                elif step == planes - 2 and order * groups + g == min(1, fold * groups - 1):
                    pass_rows()

    @pl.when(distance == planes - 1)
    def _():
        products(pieces - 1)

    for fetched in fetches[5:]:
        fetched.wait()
    for piece in range(pieces):
        chunk, h = other_part(piece // groups), piece % groups
        for g in range(groups):
            update = total[part, chunk, h, g]
            for step in range(1, fold):
                t_copy(step, chunk, h, g).wait_recv()
                update = update + inbox[step - 1, chunk, h, g]
            a, b = row * groups + g, col * block_cols + chunk * groups + h
            kept = pattern_ref[jnp.minimum(a, b), jnp.maximum(a, b)] == 1
            across = slice(g * size, (g + 1) * size)
            down = pl.ds(pl.multiple_of((chunk * groups + h) * size, size), size)
            out_ref[across, down] = prior_ref[across, down] + jnp.where(kept, update, jnp.zeros_like(update))

    for step in range(1, fold):
        for g in range(groups):
            y_copy(step, g, part).wait_send()
            for chunk in range(fold):
                for h in range(groups):
                    t_copy(step, chunk, h, g).wait_send()
    for index in range(planes // 2):
        near_copy(col, index, col).wait_send()
    for step in far_steps:
        for chunk in range(fold):
            far_copy(step, chunk, col).wait_send()
    for chunk in range(fold):
        for g in range(groups):
            for step in range(1, planes):
                x_copy(other_col(step), chunk, g, col).wait_send()
            for from_plane in range(planes):
                @pl.when((from_plane <= plane) & (plane < planes - 1))
                def _():
                    z_copy(0, from_plane, chunk, g).wait_send()

                @pl.when((from_plane >= plane) & (plane > 0))
                def _():
                    z_copy(1, from_plane, chunk, g).wait_send()


def on_device(panels, obs_of, counts, inv_var, pattern, prior):
    planes = lax.axis_size("col")
    fold = lax.axis_size("row") // planes
    groups, share, size, _ = panels.shape
    depth = size // fold
    names = -(-inv_var.shape[0] // 128) * 128
    far_memory = pl.BlockSpec(memory_space=pltpu.HBM)
    dma = pltpu.SemaphoreType.DMA
    others = max(fold - 1, 1)
    panel = (fold, groups, share, depth, size)
    turned = (fold, groups, size, share * depth)
    tile = (fold, groups, groups, size, size)
    return pl.pallas_call(
        functools.partial(kernel, planes, fold),
        out_shape=jax.ShapeDtypeStruct(prior.shape, prior.dtype),
        in_specs=[far_memory] * 6,
        out_specs=pl.BlockSpec(memory_space=pltpu.VMEM),
        scratch_shapes=[
            pltpu.SMEM(obs_of.shape, jnp.int32),
            pltpu.SMEM(counts.shape, jnp.int32),
            pltpu.SMEM(pattern.shape, jnp.int32),
            pltpu.VMEM(obs_of.shape, jnp.int32),
            pltpu.VMEM(inv_var.shape, jnp.float32),
            pltpu.VMEM(panels.shape, jnp.bfloat16),
            pltpu.VMEM(prior.shape, jnp.float32),
            pltpu.VMEM((obs_of.shape[0], names), jnp.int32),
            pltpu.SMEM((obs_of.shape[0], names), jnp.int32),
            pltpu.VMEM((size, groups * share), jnp.float32),
            pltpu.VMEM((others,) + panel[1:], jnp.bfloat16),
            pltpu.VMEM((planes,) + panel, jnp.bfloat16),
            pltpu.VMEM(turned, jnp.bfloat16),
            pltpu.VMEM((planes,) + turned, jnp.bfloat16),
            (pltpu.VMEM((obs_of.shape[1] + 1, depth, size), jnp.bfloat16),) * (fold * groups),
            pltpu.VMEM((fold,) + tile, jnp.float32),
            pltpu.VMEM((others,) + tile, jnp.float32),
            dma((others, groups)), dma((fold, groups)),
            dma((2, planes, fold, groups)), dma((planes, fold, groups)),
            dma((planes, fold, groups)), dma((planes, fold, groups)),
            dma((planes, fold)), dma((planes, fold)),
            dma((planes // 2,)), dma((planes // 2,)),
            dma((others, fold, groups, groups)), dma((others, fold, groups, groups)),
            dma((fold, groups)), dma((8,)), dma,
        ],
        compiler_params=pltpu.CompilerParams(
            collective_id=0, has_side_effects=True, vmem_limit_bytes=60 * 1024 * 1024),
    )(panels, obs_of, counts, inv_var, pattern, prior)


def solution(mesh):
    placed = (P("row", "col", None, None), P(), P(), P(), P(), P("row", "col"))
    return jax.shard_map(
        on_device, mesh=mesh, in_specs=placed, out_specs=P("row", "col"), check_vma=False
    )
```

```python
import functools

import jax
import jax.numpy as jnp
from jax import lax
from jax.experimental import pallas as pl
from jax.experimental.pallas import tpu as pltpu
from jax.sharding import PartitionSpec as P

MESH = pl.DeviceIdType.MESH


def kernel(planes, fold, source_ref, obs_source, counts_source, var_source, pattern_source, prior_source, out_ref,
           obs_ref, counts_ref, pattern_ref, ids_ref, var_ref, panels_ref, prior_ref, table, place_ref, weights, leaving, held, turned, rows, cols, total, inbox,
           y_send, y_recv, z_send, z_recv, x_send, x_recv, r_send, r_recv, n_send, n_recv,
           t_send, t_recv, keep, fetch, place_fetch):
    row, col = lax.axis_index("row"), lax.axis_index("col")
    plane, part = row // fold, row % fold
    groups, share, size = panels_ref.shape[0], panels_ref.shape[1], panels_ref.shape[2]
    depth = size // fold
    wide = share * depth
    slot_count = ids_ref.shape[1]
    near = col + 1 - 2 * lax.rem(col, 2)
    far_steps = range(2, planes, 2)

    def at(other_row, other_col):
        return {"row": other_row, "col": other_col}

    def other_plane(step):
        return lax.rem(plane + step, planes)

    def other_col(step):
        return lax.rem(col + step, planes)

    def other_part(step):
        return lax.rem(part + step, fold)

    fetches = [pltpu.make_async_copy(source, target, fetch.at[index]) for index, (source, target) in enumerate((
        (obs_source, obs_ref), (counts_source, counts_ref), (var_source, var_ref), (source_ref, panels_ref),
        (obs_source, ids_ref), (pattern_source, pattern_ref), (prior_source, prior_ref)))]
    for fetched in fetches:
        fetched.start()
    partners = [at(other_plane(s) * fold + part, col) for s in (1, planes - 1)]
    partners += [at(row, other_col(s)) for s in range(1, planes)]
    partners += [at(plane * fold + other_part(s), col) for s in range(1, fold)]
    barrier = pltpu.get_barrier_semaphore()
    for partner in partners:
        pl.semaphore_signal(barrier, inc=1, device_id=partner, device_id_type=MESH)

    for fetched in fetches[:3]:
        fetched.wait()
    factors = []
    for g in range(groups):
        block = row * groups + g
        for p in range(share):
            slot = col * share + p
            live = jnp.where(slot < counts_ref[block], 1.0, 0.0)
            factors.append(jnp.sqrt(var_ref[pl.ds(obs_ref[block, slot], 1), :]) * live)
    weights[...] = jnp.concatenate(factors, axis=0).T
    fetches[3].wait()

    def scaled(to_part, g, p):
        j = g * share + p
        lines = pl.ds(pl.multiple_of(to_part * depth, depth), depth)
        value = panels_ref[g, p, lines, :].astype(jnp.float32) * weights[lines, j:j + 1]
        return value.astype(jnp.bfloat16)

    def copy(src, dst, send, recv, device):
        return pltpu.make_async_remote_copy(
            src_ref=src, dst_ref=dst, send_sem=send, recv_sem=recv,
            device_id=device, device_id_type=MESH)

    def y_copy(step, g, landing):
        return copy(leaving.at[step - 1, g], held.at[plane, landing, g], y_send.at[step - 1, g],
                    y_recv.at[landing, g], at(plane * fold + other_part(step), col))

    def z_copy(way, from_plane, chunk, g):
        target = lax.rem(plane + (1 if way == 0 else planes - 1), planes)
        return copy(held.at[from_plane, chunk, g], held.at[from_plane, chunk, g],
                    z_send.at[way, from_plane, chunk, g], z_recv.at[from_plane, chunk, g],
                    at(target * fold + part, col))

    def slots_of(slot_col):
        return pl.ds(slot_col * share, share)

    def x_copy(to_col, order, g, landing):
        return copy(held.at[to_col, other_part(order), g], cols[order * groups + g].at[slots_of(landing)],
                    x_send.at[to_col, order, g], x_recv.at[landing, order, g], at(row, to_col))

    def keep_copy(order, g):
        return pltpu.make_async_copy(held.at[col, other_part(order), g], cols[order * groups + g].at[slots_of(col)],
                                     keep.at[order, g])

    def far_copy(step, chunk, landing):
        return copy(turned.at[chunk], rows.at[landing, chunk], r_send.at[step, chunk],
                    r_recv.at[landing, chunk], at(row, other_col(step)))

    def near_copy(slot, index, landing):
        source = turned if index == 0 else rows.at[slot]
        return copy(source, rows.at[landing], n_send.at[index], n_recv.at[index], at(row, near))

    def t_copy(step, chunk, h, g):
        return copy(total.at[other_part(step), chunk, h, g], inbox.at[step - 1, chunk, h, g],
                    t_send.at[step - 1, chunk, h, g], t_recv.at[step - 1, chunk, h, g],
                    at(plane * fold + other_part(step), col))

    def spread(from_plane, order, g):
        @pl.when(from_plane != col)
        def _():
            x_copy(from_plane, order, g, col).start()

        @pl.when(from_plane == col)
        def _():
            keep_copy(order, g).start()

    def begin(chunk, g):
        @pl.when(plane < planes - 1)
        def _():
            z_copy(0, plane, chunk, g).start()

        @pl.when(plane > 0)
        def _():
            z_copy(1, plane, chunk, g).start()

    def turn(chunk, g):
        turned[chunk, g] = held[plane, chunk, g].reshape(wide, size).T

    for step in range(1, fold):
        for g in range(groups):
            for p in range(share):
                leaving[step - 1, g, p] = scaled(other_part(step), g, p)
    pl.semaphore_wait(barrier, len(partners))
    for step in range(1, fold):
        for g in range(groups):
            y_copy(step, g, part).start()
    for g in range(groups):
        for p in range(share):
            held[plane, part, g, p] = scaled(part, g, p)
        begin(part, g)
    for g in range(groups):
        spread(plane, 0, g)
        turn(part, g)
    for step in far_steps:
        far_copy(step, part, col).start()
    for step in range(1, fold):
        for g in range(groups):
            y_copy(step, g, other_part(step)).wait_recv()
            begin(other_part(step), g)
        for g in range(groups):
            spread(plane, step, g)
            turn(other_part(step), g)
        for far in far_steps:
            far_copy(far, other_part(step), col).start()
    ids = lax.broadcasted_iota(jnp.int32, table.shape, 1)
    fetches[4].wait()
    found = jnp.full(table.shape, slot_count, jnp.int32)
    for p in range(slot_count):
        found = jnp.where(ids_ref[:, p:p + 1] == ids, p, found)
    table[...] = found
    placed = pltpu.make_async_copy(table, place_ref, place_fetch)
    placed.start()
    for piece in range(fold * groups):
        cols[piece][slot_count] = jnp.zeros((depth, size), jnp.bfloat16)
    own_row = pltpu.make_async_copy(turned, rows.at[col], fetch.at[len(fetches)])
    own_row.start()
    near_copy(col, 0, col).start()

    def pass_rows():
        for index, step in enumerate(far_steps):
            slot = other_col(step)
            for chunk in range(fold):
                far_copy(step, chunk, slot).wait_recv()
            near_copy(slot, index + 1, slot).start()

    block_cols = groups * fold
    paired = 2 if planes % 2 == 0 else 1

    def partial_tiles(step_part, piece):
        row_part, chunk, h = other_part(step_part), other_part(piece // groups), piece % groups
        b = col * block_cols + chunk * groups + h

        def step(i, unused):
            for slot_col in [i * paired + k for k in range(paired)]:
                for g in range(groups):
                    a = (plane * fold + row_part) * groups + g
                    lines = [cols[piece][place_ref[b, obs_ref[a, slot_col * share + p]]] for p in range(share)]
                    total[row_part, chunk, h, g] += jnp.dot(
                        rows[slot_col, row_part, g], jnp.concatenate(lines, axis=0),
                        preferred_element_type=jnp.float32)
            return unused

        total[row_part, chunk, h] = jnp.zeros(total.shape[3:], jnp.float32)
        lax.fori_loop(0, planes // paired, step, 0)
        if step_part > 0:
            for g in range(groups):
                t_copy(step_part, chunk, h, g).start()

    def await_rows():
        placed.wait()
        own_row.wait()
        near_copy(near, 0, near).wait_recv()
        for index, step in enumerate(far_steps):
            slot = lax.rem(near + step, planes)
            near_copy(slot, index + 1, slot).wait_recv()

    def await_columns(piece):
        order, g = piece // groups, piece % groups
        keep_copy(order, g).wait()
        for step in range(1, planes):
            x_copy(col, order, g, other_col(step)).wait_recv()

    distance = jnp.maximum(plane - col, col - plane)
    pieces = fold * groups

    at_end = (plane == 0) | (plane == planes - 1)
    own_later = at_end & (distance < planes - 1)
    own_now = jnp.logical_not(own_later)

    def products(piece):
        if piece == 0:
            await_rows()
        await_columns(piece)
        for step_part in range(1, fold):
            partial_tiles(step_part, piece)

        @pl.when(own_now)
        def _():
            partial_tiles(0, piece)

    def products_between(piece):
        @pl.when(distance < planes - 1)
        def _():
            products(piece)

        if piece > 0:
            @pl.when(distance == planes - 1)
            def _():
                products(piece - 1)

    for step in range(1, planes):
        below, above = plane - step, plane + step
        for order in range(fold):
            chunk = other_part(order)
            for g in range(groups):
                @pl.when(below >= 0)
                def _():
                    z_copy(0, below, chunk, g).wait_recv()

                    @pl.when(plane < planes - 1)
                    def _():
                        z_copy(0, below, chunk, g).start()

                    spread(below, order, g)

                @pl.when(above < planes)
                def _():
                    z_copy(1, above, chunk, g).wait_recv()

                    @pl.when(plane > 0)
                    def _():
                        z_copy(1, above, chunk, g).start()

                    spread(above, order, g)

                if step == planes - 1:
                    products_between(order * groups + g)
                elif step == planes - 2 and order * groups + g == min(1, fold * groups - 1):
                    pass_rows()

    @pl.when(distance == planes - 1)
    def _():
        products(pieces - 1)

    @pl.when(own_later)
    def _():
        for piece in range(pieces):
            partial_tiles(0, piece)

    for fetched in fetches[5:]:
        fetched.wait()
    for piece in range(pieces):
        chunk, h = other_part(piece // groups), piece % groups
        for g in range(groups):
            update = total[part, chunk, h, g]
            for step in range(1, fold):
                t_copy(step, chunk, h, g).wait_recv()
                update = update + inbox[step - 1, chunk, h, g]
            a, b = row * groups + g, col * block_cols + chunk * groups + h
            kept = pattern_ref[jnp.minimum(a, b), jnp.maximum(a, b)] == 1
            across = slice(g * size, (g + 1) * size)
            down = pl.ds(pl.multiple_of((chunk * groups + h) * size, size), size)
            out_ref[across, down] = prior_ref[across, down] + jnp.where(kept, update, jnp.zeros_like(update))

    for step in range(1, fold):
        for g in range(groups):
            y_copy(step, g, part).wait_send()
            for chunk in range(fold):
                for h in range(groups):
                    t_copy(step, chunk, h, g).wait_send()
    for index in range(planes // 2):
        near_copy(col, index, col).wait_send()
    for step in far_steps:
        for chunk in range(fold):
            far_copy(step, chunk, col).wait_send()
    for chunk in range(fold):
        for g in range(groups):
            for step in range(1, planes):
                x_copy(other_col(step), chunk, g, col).wait_send()
            for from_plane in range(planes):
                @pl.when((from_plane <= plane) & (plane < planes - 1))
                def _():
                    z_copy(0, from_plane, chunk, g).wait_send()

                @pl.when((from_plane >= plane) & (plane > 0))
                def _():
                    z_copy(1, from_plane, chunk, g).wait_send()


def on_device(panels, obs_of, counts, inv_var, pattern, prior):
    planes = lax.axis_size("col")
    fold = lax.axis_size("row") // planes
    groups, share, size, _ = panels.shape
    depth = size // fold
    names = -(-inv_var.shape[0] // 128) * 128
    far_memory = pl.BlockSpec(memory_space=pltpu.HBM)
    dma = pltpu.SemaphoreType.DMA
    others = max(fold - 1, 1)
    panel = (fold, groups, share, depth, size)
    turned = (fold, groups, size, share * depth)
    tile = (fold, groups, groups, size, size)
    return pl.pallas_call(
        functools.partial(kernel, planes, fold),
        out_shape=jax.ShapeDtypeStruct(prior.shape, prior.dtype),
        in_specs=[far_memory] * 6,
        out_specs=pl.BlockSpec(memory_space=pltpu.VMEM),
        scratch_shapes=[
            pltpu.SMEM(obs_of.shape, jnp.int32),
            pltpu.SMEM(counts.shape, jnp.int32),
            pltpu.SMEM(pattern.shape, jnp.int32),
            pltpu.VMEM(obs_of.shape, jnp.int32),
            pltpu.VMEM(inv_var.shape, jnp.float32),
            pltpu.VMEM(panels.shape, jnp.bfloat16),
            pltpu.VMEM(prior.shape, jnp.float32),
            pltpu.VMEM((obs_of.shape[0], names), jnp.int32),
            pltpu.SMEM((obs_of.shape[0], names), jnp.int32),
            pltpu.VMEM((size, groups * share), jnp.float32),
            pltpu.VMEM((others,) + panel[1:], jnp.bfloat16),
            pltpu.VMEM((planes,) + panel, jnp.bfloat16),
            pltpu.VMEM(turned, jnp.bfloat16),
            pltpu.VMEM((planes,) + turned, jnp.bfloat16),
            (pltpu.VMEM((obs_of.shape[1] + 1, depth, size), jnp.bfloat16),) * (fold * groups),
            pltpu.VMEM((fold,) + tile, jnp.float32),
            pltpu.VMEM((others,) + tile, jnp.float32),
            dma((others, groups)), dma((fold, groups)),
            dma((2, planes, fold, groups)), dma((planes, fold, groups)),
            dma((planes, fold, groups)), dma((planes, fold, groups)),
            dma((planes, fold)), dma((planes, fold)),
            dma((planes // 2,)), dma((planes // 2,)),
            dma((others, fold, groups, groups)), dma((others, fold, groups, groups)),
            dma((fold, groups)), dma((8,)), dma,
        ],
        compiler_params=pltpu.CompilerParams(
            collective_id=0, has_side_effects=True, vmem_limit_bytes=60 * 1024 * 1024),
    )(panels, obs_of, counts, inv_var, pattern, prior)


def solution(mesh):
    placed = (P("row", "col", None, None), P(), P(), P(), P(), P("row", "col"))
    return jax.shard_map(
        on_device, mesh=mesh, in_specs=placed, out_specs=P("row", "col"), check_vma=False
    )
```

```python
import functools

import jax
import jax.numpy as jnp
from jax import lax
from jax.experimental import pallas as pl
from jax.experimental.pallas import tpu as pltpu
from jax.sharding import PartitionSpec as P

MESH = pl.DeviceIdType.MESH


def kernel(planes, fold, source_ref, obs_source, counts_source, var_source, pattern_source, prior_source, out_ref,
           obs_ref, counts_ref, pattern_ref, ids_ref, var_ref, panels_ref, prior_ref, table, place_ref, weights, leaving, held, turned, rows, cols, total, inbox,
           y_send, y_recv, z_send, z_recv, x_send, x_recv, r_send, r_recv, n_send, n_recv,
           t_send, t_recv, keep, fetch, place_fetch):
    row, col = lax.axis_index("row"), lax.axis_index("col")
    plane, part = row // fold, row % fold
    groups, share, size = panels_ref.shape[0], panels_ref.shape[1], panels_ref.shape[2]
    depth = size // fold
    wide = share * depth
    slot_count = ids_ref.shape[1]
    near = col + 1 - 2 * lax.rem(col, 2)
    far_steps = range(2, planes, 2)

    def at(other_row, other_col):
        return {"row": other_row, "col": other_col}

    def other_plane(step):
        return lax.rem(plane + step, planes)

    def other_col(step):
        return lax.rem(col + step, planes)

    def other_part(step):
        return lax.rem(part + step, fold)

    fetches = [pltpu.make_async_copy(source, target, fetch.at[index]) for index, (source, target) in enumerate((
        (obs_source, obs_ref), (counts_source, counts_ref), (var_source, var_ref), (source_ref, panels_ref),
        (obs_source, ids_ref), (pattern_source, pattern_ref), (prior_source, prior_ref)))]
    for fetched in fetches:
        fetched.start()
    partners = [at(other_plane(s) * fold + part, col) for s in (1, planes - 1)]
    partners += [at(row, other_col(s)) for s in range(1, planes)]
    partners += [at(plane * fold + other_part(s), col) for s in range(1, fold)]
    barrier = pltpu.get_barrier_semaphore()
    for partner in partners:
        pl.semaphore_signal(barrier, inc=1, device_id=partner, device_id_type=MESH)

    for fetched in fetches[:3]:
        fetched.wait()
    factors = []
    for g in range(groups):
        block = row * groups + g
        for p in range(share):
            slot = col * share + p
            live = jnp.where(slot < counts_ref[block], 1.0, 0.0)
            factors.append(jnp.sqrt(var_ref[pl.ds(obs_ref[block, slot], 1), :]) * live)
    weights[...] = jnp.concatenate(factors, axis=0).T
    fetches[3].wait()

    def scaled(to_part, g, p):
        j = g * share + p
        lines = pl.ds(pl.multiple_of(to_part * depth, depth), depth)
        value = panels_ref[g, p, lines, :].astype(jnp.float32) * weights[lines, j:j + 1]
        return value.astype(jnp.bfloat16)

    def copy(src, dst, send, recv, device):
        return pltpu.make_async_remote_copy(
            src_ref=src, dst_ref=dst, send_sem=send, recv_sem=recv,
            device_id=device, device_id_type=MESH)

    def y_copy(step, g, landing):
        return copy(leaving.at[step - 1, g], held.at[plane, landing, g], y_send.at[step - 1, g],
                    y_recv.at[landing, g], at(plane * fold + other_part(step), col))

    def z_copy(way, from_plane, chunk, g):
        target = lax.rem(plane + (1 if way == 0 else planes - 1), planes)
        return copy(held.at[from_plane, chunk, g], held.at[from_plane, chunk, g],
                    z_send.at[way, from_plane, chunk, g], z_recv.at[from_plane, chunk, g],
                    at(target * fold + part, col))

    def slots_of(slot_col):
        return pl.ds(slot_col * share, share)

    def x_copy(to_col, order, g, landing):
        return copy(held.at[to_col, other_part(order), g], cols[order * groups + g].at[slots_of(landing)],
                    x_send.at[to_col, order, g], x_recv.at[landing, order, g], at(row, to_col))

    def keep_copy(order, g):
        return pltpu.make_async_copy(held.at[col, other_part(order), g], cols[order * groups + g].at[slots_of(col)],
                                     keep.at[order, g])

    def far_copy(step, chunk, landing):
        return copy(turned.at[chunk], rows.at[landing, chunk], r_send.at[step, chunk],
                    r_recv.at[landing, chunk], at(row, other_col(step)))

    def near_copy(slot, index, landing):
        source = turned if index == 0 else rows.at[slot]
        return copy(source, rows.at[landing], n_send.at[index], n_recv.at[index], at(row, near))

    def t_copy(step, chunk, h, g):
        return copy(total.at[other_part(step), chunk, h, g], inbox.at[step - 1, chunk, h, g],
                    t_send.at[step - 1, chunk, h, g], t_recv.at[step - 1, chunk, h, g],
                    at(plane * fold + other_part(step), col))

    def spread(from_plane, order, g):
        @pl.when(from_plane != col)
        def _():
            x_copy(from_plane, order, g, col).start()

        @pl.when(from_plane == col)
        def _():
            keep_copy(order, g).start()

    def begin(chunk, g):
        @pl.when(plane < planes - 1)
        def _():
            z_copy(0, plane, chunk, g).start()

        @pl.when(plane > 0)
        def _():
            z_copy(1, plane, chunk, g).start()

    def turn(chunk, g):
        turned[chunk, g] = held[plane, chunk, g].reshape(wide, size).T

    for step in range(1, fold):
        for g in range(groups):
            for p in range(share):
                leaving[step - 1, g, p] = scaled(other_part(step), g, p)
    pl.semaphore_wait(barrier, len(partners))
    for step in range(1, fold):
        for g in range(groups):
            y_copy(step, g, part).start()
    for g in range(groups):
        for p in range(share):
            held[plane, part, g, p] = scaled(part, g, p)
        begin(part, g)
    for g in range(groups):
        spread(plane, 0, g)
        turn(part, g)
    for step in far_steps:
        far_copy(step, part, col).start()
    for step in range(1, fold):
        for g in range(groups):
            y_copy(step, g, other_part(step)).wait_recv()
            begin(other_part(step), g)
        for g in range(groups):
            spread(plane, step, g)
            turn(other_part(step), g)
        for far in far_steps:
            far_copy(far, other_part(step), col).start()
    ids = lax.broadcasted_iota(jnp.int32, table.shape, 1)
    fetches[4].wait()
    found = jnp.full(table.shape, slot_count, jnp.int32)
    for p in range(slot_count):
        found = jnp.where(ids_ref[:, p:p + 1] == ids, p, found)
    table[...] = found
    placed = pltpu.make_async_copy(table, place_ref, place_fetch)
    placed.start()
    for piece in range(fold * groups):
        cols[piece][slot_count] = jnp.zeros((depth, size), jnp.bfloat16)
    own_row = pltpu.make_async_copy(turned, rows.at[col], fetch.at[len(fetches)])
    own_row.start()
    near_copy(col, 0, col).start()

    def pass_rows():
        for index, step in enumerate(far_steps):
            slot = other_col(step)
            for chunk in range(fold):
                far_copy(step, chunk, slot).wait_recv()
            near_copy(slot, index + 1, slot).start()

    block_cols = groups * fold
    paired = 2 if planes % 2 == 0 else 1

    def partial_tiles(step_part, piece):
        row_part, chunk, h = other_part(step_part), other_part(piece // groups), piece % groups
        b = col * block_cols + chunk * groups + h

        def step(i, unused):
            for slot_col in [i * paired + k for k in range(paired)]:
                for g in range(groups):
                    a = (plane * fold + row_part) * groups + g
                    lines = [cols[piece][place_ref[b, obs_ref[a, slot_col * share + p]]] for p in range(share)]
                    total[row_part, chunk, h, g] += jnp.dot(
                        rows[slot_col, row_part, g], jnp.concatenate(lines, axis=0),
                        preferred_element_type=jnp.float32)
            return unused

        total[row_part, chunk, h] = jnp.zeros(total.shape[3:], jnp.float32)
        lax.fori_loop(0, planes // paired, step, 0)
        if step_part > 0:
            for g in range(groups):
                t_copy(step_part, chunk, h, g).start()

    def await_rows():
        placed.wait()
        own_row.wait()
        near_copy(near, 0, near).wait_recv()
        for index, step in enumerate(far_steps):
            slot = lax.rem(near + step, planes)
            near_copy(slot, index + 1, slot).wait_recv()

    def await_columns(piece):
        order, g = piece // groups, piece % groups
        keep_copy(order, g).wait()
        for step in range(1, planes):
            x_copy(col, order, g, other_col(step)).wait_recv()

    distance = jnp.maximum(plane - col, col - plane)
    pieces = fold * groups

    def products(piece):
        if piece == 0:
            await_rows()
        await_columns(piece)
        for step_part in range(1, fold):
            partial_tiles(step_part, piece)
        partial_tiles(0, piece)

    def products_between(piece):
        @pl.when(distance < planes - 1)
        def _():
            products(piece)

        if piece > 0:
            @pl.when(distance == planes - 1)
            def _():
                products(piece - 1)

    for step in range(1, planes):
        below, above = plane - step, plane + step
        for order in range(fold):
            chunk = other_part(order)
            for g in range(groups):
                @pl.when(below >= 0)
                def _():
                    z_copy(0, below, chunk, g).wait_recv()

                    @pl.when(plane < planes - 1)
                    def _():
                        z_copy(0, below, chunk, g).start()

                    spread(below, order, g)

                @pl.when(above < planes)
                def _():
                    z_copy(1, above, chunk, g).wait_recv()

                    @pl.when(plane > 0)
                    def _():
                        z_copy(1, above, chunk, g).start()

                    spread(above, order, g)

                if step == planes - 1:
                    products_between(order * groups + g)
                elif step == planes - 2 and order * groups + g == fold * groups - 1:
                    pass_rows()

    @pl.when(distance == planes - 1)
    def _():
        products(pieces - 1)

    for fetched in fetches[5:]:
        fetched.wait()
    for piece in range(pieces):
        chunk, h = other_part(piece // groups), piece % groups
        for g in range(groups):
            update = total[part, chunk, h, g]
            for step in range(1, fold):
                t_copy(step, chunk, h, g).wait_recv()
                update = update + inbox[step - 1, chunk, h, g]
            a, b = row * groups + g, col * block_cols + chunk * groups + h
            kept = pattern_ref[jnp.minimum(a, b), jnp.maximum(a, b)] == 1
            across = slice(g * size, (g + 1) * size)
            down = pl.ds(pl.multiple_of((chunk * groups + h) * size, size), size)
            out_ref[across, down] = prior_ref[across, down] + jnp.where(kept, update, jnp.zeros_like(update))

    for step in range(1, fold):
        for g in range(groups):
            y_copy(step, g, part).wait_send()
            for chunk in range(fold):
                for h in range(groups):
                    t_copy(step, chunk, h, g).wait_send()
    for index in range(planes // 2):
        near_copy(col, index, col).wait_send()
    for step in far_steps:
        for chunk in range(fold):
            far_copy(step, chunk, col).wait_send()
    for chunk in range(fold):
        for g in range(groups):
            for step in range(1, planes):
                x_copy(other_col(step), chunk, g, col).wait_send()
            for from_plane in range(planes):
                @pl.when((from_plane <= plane) & (plane < planes - 1))
                def _():
                    z_copy(0, from_plane, chunk, g).wait_send()

                @pl.when((from_plane >= plane) & (plane > 0))
                def _():
                    z_copy(1, from_plane, chunk, g).wait_send()


def on_device(panels, obs_of, counts, inv_var, pattern, prior):
    planes = lax.axis_size("col")
    fold = lax.axis_size("row") // planes
    groups, share, size, _ = panels.shape
    depth = size // fold
    names = -(-inv_var.shape[0] // 128) * 128
    far_memory = pl.BlockSpec(memory_space=pltpu.HBM)
    dma = pltpu.SemaphoreType.DMA
    others = max(fold - 1, 1)
    panel = (fold, groups, share, depth, size)
    turned = (fold, groups, size, share * depth)
    tile = (fold, groups, groups, size, size)
    return pl.pallas_call(
        functools.partial(kernel, planes, fold),
        out_shape=jax.ShapeDtypeStruct(prior.shape, prior.dtype),
        in_specs=[far_memory] * 6,
        out_specs=pl.BlockSpec(memory_space=pltpu.VMEM),
        scratch_shapes=[
            pltpu.SMEM(obs_of.shape, jnp.int32),
            pltpu.SMEM(counts.shape, jnp.int32),
            pltpu.SMEM(pattern.shape, jnp.int32),
            pltpu.VMEM(obs_of.shape, jnp.int32),
            pltpu.VMEM(inv_var.shape, jnp.float32),
            pltpu.VMEM(panels.shape, jnp.bfloat16),
            pltpu.VMEM(prior.shape, jnp.float32),
            pltpu.VMEM((obs_of.shape[0], names), jnp.int32),
            pltpu.SMEM((obs_of.shape[0], names), jnp.int32),
            pltpu.VMEM((size, groups * share), jnp.float32),
            pltpu.VMEM((others,) + panel[1:], jnp.bfloat16),
            pltpu.VMEM((planes,) + panel, jnp.bfloat16),
            pltpu.VMEM(turned, jnp.bfloat16),
            pltpu.VMEM((planes,) + turned, jnp.bfloat16),
            (pltpu.VMEM((obs_of.shape[1] + 1, depth, size), jnp.bfloat16),) * (fold * groups),
            pltpu.VMEM((fold,) + tile, jnp.float32),
            pltpu.VMEM((others,) + tile, jnp.float32),
            dma((others, groups)), dma((fold, groups)),
            dma((2, planes, fold, groups)), dma((planes, fold, groups)),
            dma((planes, fold, groups)), dma((planes, fold, groups)),
            dma((planes, fold)), dma((planes, fold)),
            dma((planes // 2,)), dma((planes // 2,)),
            dma((others, fold, groups, groups)), dma((others, fold, groups, groups)),
            dma((fold, groups)), dma((8,)), dma,
        ],
        compiler_params=pltpu.CompilerParams(
            collective_id=0, has_side_effects=True, vmem_limit_bytes=60 * 1024 * 1024),
    )(panels, obs_of, counts, inv_var, pattern, prior)


def solution(mesh):
    placed = (P("row", "col", None, None), P(), P(), P(), P(), P("row", "col"))
    return jax.shard_map(
        on_device, mesh=mesh, in_specs=placed, out_specs=P("row", "col"), check_vma=False
    )
```
